256 devices in a mesh: frames: 8 (over z_lo, y), patch: 32 (over x, z_hi, core).
Axes of the slice: x: 4, y: 4, z: 8 (z_hi: 4, z_lo: 2; z = z_hi * 2 + z_lo), core: 2. Of those that a mesh axis runs over, the one named last changes fastest.
Arguments:
- object_band: float32 [2048, 256], P('patch'), may hold values from -6 to 6
- data_band: float32 [2048, 16, 256], P('patch', 'frames'), may hold values from -6 to 6
- coeffs: float32 [16, 32, 4, 200], P('frames', 'patch'), may hold values from -5 to 5
- mode_basis: float32 [200, 2304], replicated, may hold values from -0.4375 to 0.4375
- offsets: int32 [32, 4, 2], P('patch'), may hold values from 0 to 16
- window_ids: int32 [32, 4], P('patch'), may hold values from 0 to 3
- counts: int32 [32], P('patch'), may hold values from 2 to 4, as said below
Outputs:
- object_grad: float32 [2048, 256], P('patch')
- coeff_grad: float32 [16, 32, 4, 200], P('frames', 'patch')
The draws below stay inside these ranges and needn't reach their ends.
Inputs may be any that keep to these rules, and one draw needn't show every extreme that they name: Patch row r holds its first counts[r] patches inside the image; some patch row holds all 4 and some only 2.
All inputs are finite; a program needn't handle non-finite values.
Results may differ from the reference program's by a relative error of at most 0.0003.
Values sent between devices are 32-bit elements; how exact they have to be, the bound alone decides.
No kernel may reach another device: no remote copies, remote signals or barrier semaphores. Data moves between devices by JAX's collectives and lax.ppermute only.
A program may use at most 64 MiB of HBM per device.

```python
import math
import jax
import jax.numpy as jnp
from jax import lax

PP = 96
PU = 48
MODES = 200
STRIDE = 64
HALO = 24
OFFMAX = 16
PC = 4
FR = 16
PROWS = 32
NROWS = 2048
NCOLS = 256


def draw_counts(key, part):
    key = jax.random.fold_in(key, 7)
    first, second = jax.random.split(key)
    drawn = jax.random.randint(first, (PROWS,), PC // 2, PC + 1)
    order_ids = jax.random.permutation(second, PROWS)
    drawn = jnp.where(order_ids == 0, PC, drawn)
    return jnp.where(order_ids == 1, PC // 2, drawn).astype(jnp.int32)


def place_ends(entries, own_key, low, high):
    index_at = [jax.random.randint(jax.random.fold_in(own_key, axis), (), 0, length) for axis, length in enumerate(entries.shape)]
    main_axis = entries.shape.index(max(entries.shape))
    beside = index_at[:main_axis] + [(index_at[main_axis] + 1) % entries.shape[main_axis]] + index_at[main_axis + 1:]
    return entries.at[tuple(index_at)].set(low).at[tuple(beside)].set(high)


def steps_of(rng, dims, shards, least, high):
    loudness, own = 1.0, jax.random.fold_in(rng, 6)
    for dim, parts in shards:
        steps = jnp.exp(jax.random.uniform(jax.random.fold_in(own, dim), (parts,), jnp.float32, least / len(shards), high / len(shards)))
        loudness = loudness * jnp.repeat(steps, dims[dim] // parts).reshape([-1 if axis == dim else 1 for axis in range(len(dims))])
    return loudness


def bell_draw(stream_key, shape, deviation, reach, shards=(), kind=jnp.bfloat16):
    factor_of = steps_of(stream_key, shape, shards, -0.22, 0.18) if shards else 1.0
    values = jax.random.normal(stream_key, shape, jnp.float32) * deviation * factor_of
    return jnp.minimum(jnp.maximum(values, -reach), reach).astype(kind)


def setup_inputs(seed: int = 0) -> dict:
    seeds = jax.random.split(jax.random.key(seed), 8)
    return {
        "object_band": bell_draw(seeds[0], (NROWS, NCOLS), 1.0, 6.0, ((0, 32),), jnp.float32),
        "data_band": bell_draw(seeds[1], (NROWS, FR, NCOLS), 1.0, 6.0, ((0, 32), (1, 8)), jnp.float32),
        "coeffs": bell_draw(seeds[2], (FR, PROWS, PC, MODES), 1.0, 5.0, ((0, 8), (1, 32)), jnp.float32),
        "mode_basis": bell_draw(seeds[3], (MODES, PU * PU), MODES ** -0.5, 0.4375, (), jnp.float32),
        "offsets": place_ends(jax.random.randint(seeds[4], (PROWS, PC, 2), 0, OFFMAX + 1), jax.random.fold_in(seeds[4], 1), 0, OFFMAX).astype(jnp.int32),
        "window_ids": place_ends(jax.random.randint(seeds[5], (PROWS, PC), 0, 4), jax.random.fold_in(seeds[5], 1), 0, 3).astype(jnp.int32),
        "counts": draw_counts(jax.random.fold_in(seeds[7], 71), 0),
    }


PRECISE = lax.Precision.HIGHEST

def dft_pair(points, length):
    row_ids = jnp.arange(points, dtype=jnp.int32)[:, None]
    col_ids = jnp.arange(length, dtype=jnp.int32)[None, :]
    angles = 2.0 * math.pi / points * (row_ids * col_ids % points).astype(jnp.float32)
    return (jnp.cos(angles), -jnp.sin(angles))

def window_set(side):
    cell_pos = jnp.arange(side, dtype=jnp.float32) + 0.5
    profiles = []
    for taper_kind in range(4):
        edge_width = float(max(side * (taper_kind + 1) // 12, 1))
        rising = 0.5 - 0.5 * jnp.cos(math.pi * jnp.minimum(cell_pos, edge_width) / edge_width)
        profile = rising * rising[::-1]
        profiles.append(profile[:, None] * profile[None, :])
    return jnp.stack(profiles)

def aperture(side):
    centre = jnp.arange(side, dtype=jnp.float32) + 0.5 - 0.5 * side
    radius_sq = centre[:, None] ** 2 + centre[None, :] ** 2
    return (radius_sq <= (0.5 * side) ** 2).astype(jnp.float32)

def rows_by(matrix, field):
    return jnp.einsum('ux,...xy->...uy', matrix, field, precision=PRECISE)

def cols_by(field, matrix):
    return jnp.einsum('...uy,vy->...uv', field, matrix, precision=PRECISE)

def forward_real(field, full_re, full_im):
    mixed_re = rows_by(full_re, field)
    mixed_im = rows_by(full_im, field)
    out_re = cols_by(mixed_re, full_re) - cols_by(mixed_im, full_im)
    out_im = cols_by(mixed_re, full_im) + cols_by(mixed_im, full_re)
    return (out_re, out_im)

def inverse_real(spec_re, spec_im, full_re, full_im):
    back_re = rows_by(full_re, spec_re) + rows_by(full_im, spec_im)
    back_im = rows_by(full_re, spec_im) - rows_by(full_im, spec_re)
    return (cols_by(back_re, full_re) + cols_by(back_im, full_im)) / float(PP * PP)

def patch_misfit(obj_patches, coeff_rows, data_patches, windows, usable, mode_basis):
    full_re, full_im = dft_pair(PP, PP)
    half_re, half_im = dft_pair(PP, PU)
    wavefront = jnp.einsum('fpm,mk->fpk', coeff_rows, mode_basis, precision=PRECISE)
    wavefront = wavefront.reshape(coeff_rows.shape[0], coeff_rows.shape[1], PU, PU)
    opening = aperture(PU)
    pupil_re = opening * jnp.cos(wavefront)
    pupil_im = opening * jnp.sin(wavefront)
    left_re = rows_by(half_re, pupil_re) - rows_by(half_im, pupil_im)
    left_im = rows_by(half_re, pupil_im) + rows_by(half_im, pupil_re)
    field_re = cols_by(left_re, half_re) - cols_by(left_im, half_im)
    field_im = cols_by(left_re, half_im) + cols_by(left_im, half_re)
    intensity = field_re * field_re + field_im * field_im
    spread = intensity / lax.optimization_barrier(jnp.sum(intensity, axis=(2, 3), keepdims=True))
    spec_re, spec_im = forward_real(spread, full_re, full_im)
    object_re, object_im = forward_real(windows * obj_patches, full_re, full_im)
    prod_re = object_re * spec_re - object_im * spec_im
    prod_im = object_re * spec_im + object_im * spec_re
    predicted = inverse_real(prod_re, prod_im, full_re, full_im)
    residual = predicted - windows * data_patches
    per_patch = lax.optimization_barrier(jnp.sum(residual * residual, axis=(0, 2, 3)))
    return 0.5 * jnp.sum(usable * per_patch)

def reference(object_band, data_band, coeffs, mode_basis, offsets, window_ids, counts):
    profiles = window_set(PP)
    obj_pad = jnp.pad(object_band, ((HALO, HALO), (HALO, HALO)))
    data_pad = jnp.pad(data_band, ((HALO, HALO), (0, 0), (HALO, HALO)))
    column = jnp.arange(PC, dtype=jnp.int32)
    kinds = jnp.arange(4, dtype=jnp.int32)

    def one_row(row_id):
        shifts = offsets[row_id]
        row_start = (row_id * STRIDE + shifts[:, 0]).astype(jnp.int32)
        col_start = (column * STRIDE + shifts[:, 1]).astype(jnp.int32)

        def cut_object(row_at, col_at):
            return lax.dynamic_slice(obj_pad, (row_at, col_at), (PP, PP))

        def cut_data(row_at, col_at):
            return lax.dynamic_slice(data_pad, (row_at, jnp.int32(0), col_at), (PP, FR, PP))
        obj_patches = jax.vmap(cut_object)(row_start, col_start)
        data_patches = jnp.transpose(jax.vmap(cut_data)(row_start, col_start), (2, 0, 1, 3))
        selector = (window_ids[row_id][:, None] == kinds[None, :]).astype(jnp.float32)
        windows = jnp.einsum('pv,vij->pij', selector, profiles, precision=PRECISE)
        usable = (column < counts[row_id]).astype(jnp.float32)

        def misfit_of(patches_now, coeffs_now):
            return patch_misfit(patches_now, coeffs_now, data_patches, windows, usable, mode_basis)
        misfit, pullback = jax.vjp(misfit_of, obj_patches, coeffs[:, row_id])
        grad_obj, grad_coef = pullback(jnp.ones((), misfit.dtype))
        return (grad_obj, grad_coef, row_start, col_start)
    grad_obj, grad_coef, row_starts, col_starts = lax.map(one_row, jnp.arange(PROWS, dtype=jnp.int32))
    flat_obj = grad_obj.reshape(PROWS * PC, PP, PP)
    flat_rows = row_starts.reshape(PROWS * PC)
    flat_cols = col_starts.reshape(PROWS * PC)

    def add_patch(which_patch, summed_grad):
        corner = (flat_rows[which_patch], flat_cols[which_patch])
        placed = lax.dynamic_slice(summed_grad, corner, (PP, PP))
        return lax.dynamic_update_slice(summed_grad, placed + flat_obj[which_patch], corner)
    summed_grad = lax.fori_loop(0, PROWS * PC, add_patch, jnp.zeros_like(obj_pad))
    object_grad = summed_grad[HALO:HALO + NROWS, HALO:HALO + NCOLS]
    coeff_grad = jnp.transpose(grad_coef, (1, 0, 2, 3))
    return (object_grad, coeff_grad)
```

```python
import math

import jax
import jax.numpy as jnp
import ml_dtypes
import numpy as np
from jax import lax
from jax.experimental import pallas as pl
from jax.experimental.pallas import tpu as pltpu
from jax.sharding import PartitionSpec as P

PP = 96
PU = 48
STRIDE = 64
HALO = 24
PC = 4
FK = 2
NI = PC * FK
LANES = 128
MODES = 200
TALL = PP + 8
HEIGHT = STRIDE + 2 * HALO + 8
F32 = jnp.float32
BF16 = jnp.bfloat16
VMEM_LIMIT = 56 * 1024 * 1024


def halves(matrix):
    high = matrix.astype(ml_dtypes.bfloat16)
    low = (matrix - high.astype(np.float64)).astype(ml_dtypes.bfloat16)
    return high, low


def dft(points, length):
    turns = np.outer(np.arange(points), np.arange(length)) % points
    angles = 2.0 * math.pi / points * turns
    return np.cos(angles), -np.sin(angles)


def constants():
    full_re, full_im = dft(PP, PP)
    half_re, half_im = dft(PP, PU)
    fwd_right = np.zeros((256, 256))
    fwd_right[:96, :96] = full_re
    fwd_right[128:224, :96] = -full_im
    fwd_right[:96, 128:224] = full_im
    fwd_right[128:224, 128:224] = full_re
    inv_right = np.zeros((256, 256))
    inv_right[:96, :96] = full_re
    inv_right[128:224, :96] = full_im
    inv_right[:96, 128:224] = -full_im
    inv_right[128:224, 128:224] = full_re
    pupil_right = np.zeros((128, 256))
    pupil_right[:48, :96] = half_re.T
    pupil_right[64:112, :96] = -half_im.T
    pupil_right[:48, 128:224] = half_im.T
    pupil_right[64:112, 128:224] = half_re.T
    pupil_left = np.block([[half_re, -half_im], [half_im, half_re]])
    fwd_left = np.block([[full_re, -full_im], [full_im, full_re]])
    inv_left = np.block([[full_re, full_im], [-full_im, full_re]])
    real_left = np.concatenate([full_re, full_im], axis=0)

    def stack(matrix):
        return np.concatenate(halves(matrix), axis=0)

    def twice(matrix):
        high, low = halves(matrix)
        return np.concatenate([high, low], axis=1)

    side = np.arange(PP) + 0.5
    windows = np.zeros((4, PP, LANES), np.float32)
    for kind in range(4):
        edge = float(max(PP * (kind + 1) // 12, 1))
        rising = 0.5 - 0.5 * np.cos(math.pi * np.minimum(side, edge) / edge)
        profile = rising * rising[::-1]
        windows[kind, :, :PP] = np.outer(profile, profile)
    centre = np.arange(PU) + 0.5 - 0.5 * PU
    opening = (centre[:, None] ** 2 + centre[None, :] ** 2 <= (0.5 * PU) ** 2).reshape(1, PU * PU)
    return {
        "fwd_right": stack(fwd_right),
        "inv_right": stack(inv_right),
        "pupil_right": stack(pupil_right),
        "pupil_left": twice(pupil_left),
        "fwd_left": stack(fwd_left),
        "inv_left": stack(inv_left),
        "real_left": twice(real_left),
        "part_left": stack(inv_left[:PP]),
        "back_left": stack(pupil_left.T.copy()),
        "back_right": stack(pupil_right.T.copy()),
        "windows": windows,
        "opening": opening.astype(np.float32),
    }


def split(values):
    high = values.astype(BF16)
    return high, (values - high.astype(F32)).astype(BF16)


def mm(a, b):
    return jnp.dot(a, b, preferred_element_type=F32)


def right(values, matrix_ref):
    depth = matrix_ref.shape[0] // 2
    rows = values.shape[0]
    high, low = split(values)
    both = mm(jnp.concatenate([high, low], axis=0), matrix_ref[:depth])
    return both[:rows] + both[rows:] + mm(high, matrix_ref[depth:])


def left(matrix_ref, values):
    rows = matrix_ref.shape[0] // 2
    high, low = split(values)
    both = mm(matrix_ref[...], high)
    return both[:rows] + both[rows:] + mm(matrix_ref[:rows], low)


def left_wide(matrix_ref, values):
    depth = values.shape[0]
    high, low = split(values)
    return mm(matrix_ref[...], jnp.concatenate([high, high], axis=0)) + mm(matrix_ref[:, :depth], low)


def to_rows(spectrum):
    parts = []
    for c in range(PC):
        lanes = slice(c * LANES, (c + 1) * LANES)
        parts.append(jnp.concatenate([spectrum[:PP, lanes], spectrum[PP:, lanes]], axis=1))
    return jnp.concatenate(parts, axis=0)


def to_lanes(rows):
    re = jnp.concatenate([rows[c * PP : (c + 1) * PP, :LANES] for c in range(PC)], axis=1)
    im = jnp.concatenate([rows[c * PP : (c + 1) * PP, LANES:] for c in range(PC)], axis=1)
    return jnp.concatenate([re, im], axis=0)


def sin_cos(angle):
    turns = jnp.floor(angle * (2.0 / math.pi) + 0.5)
    rest = angle - turns * 1.5703125
    rest = rest - turns * 4.837512969970703125e-4
    rest = rest - turns * 7.54978995489188216e-8
    sq = rest * rest
    sine = ((-1.9515295891e-4 * sq + 8.3321608736e-3) * sq - 1.6666654611e-1) * sq * rest + rest
    cosine = ((2.443315711809948e-5 * sq - 1.388731625493765e-3) * sq + 4.166664568298827e-2) * sq * sq - 0.5 * sq + 1.0
    quarter = turns.astype(jnp.int32) & 3
    swapped = (quarter & 1) == 1
    sin_now = jnp.where(swapped, cosine, sine)
    cos_now = jnp.where(swapped, sine, cosine)
    sin_now = jnp.where(quarter >= 2, -sin_now, sin_now)
    cos_now = jnp.where((quarter == 1) | (quarter == 2), -cos_now, cos_now)
    return sin_now, cos_now


def pack_kernel(object_ref, data_ref, on_ref, off_ref):
    even = lax.axis_index("patch") % 2 == 0
    low, high = STRIDE - HALO, 0
    on_at = pl.multiple_of(jnp.where(even, low, high), 8)
    off_at = pl.multiple_of(jnp.where(even, high, low), 8)
    for ref, at in ((on_ref, on_at), (off_ref, off_at)):
        ref[0:HALO, :] = object_ref[pl.ds(at, HALO), :]
        for k in range(FK):
            ref[(k + 1) * HALO : (k + 2) * HALO, :] = data_ref[pl.ds(at, HALO), k, :]


def psf_kernel(coeffs_ref, basis_ref, opening_ref, pr_ref, pl_ref, fl_ref, fr_ref,
               pupil_ref, field_ref, spec_ref, scale_ref, rows_scr, left_scr):
    coeffs = jnp.concatenate([coeffs_ref[0, 0], coeffs_ref[1, 0]], axis=0)
    c_high = coeffs.astype(BF16)
    rest = coeffs - c_high.astype(F32)
    c_mid = rest.astype(BF16)
    c_low = (rest - c_mid.astype(F32)).astype(BF16)
    basis = basis_ref[...]
    b_high = basis.astype(BF16)
    b_rest = basis - b_high.astype(F32)
    b_mid = b_rest.astype(BF16)
    b_low = (b_rest - b_mid.astype(F32)).astype(BF16)
    wave = (mm(c_high, b_low) + mm(c_mid, b_mid) + mm(c_low, b_high)) + (mm(c_high, b_mid) + mm(c_mid, b_high)) + mm(c_high, b_high)
    sine, cosine = sin_cos(wave)
    opening = opening_ref[...]
    re = cosine * opening
    im = sine * opening
    pupil_ref[...] = jnp.zeros_like(pupil_ref)
    for a in range(PU):
        pupil_ref[a * NI : (a + 1) * NI, 0:PU] = re[:, a * PU : (a + 1) * PU]
        pupil_ref[a * NI : (a + 1) * NI, 64 : 64 + PU] = im[:, a * PU : (a + 1) * PU]
    mixed = right(pupil_ref[...], pr_ref)
    rows_scr[0] = mixed[:, :LANES]
    rows_scr[1] = mixed[:, LANES:]
    for n in range(NI):
        lanes = slice(n * LANES, (n + 1) * LANES)
        left_scr[0:PU, lanes] = rows_scr[0, pl.ds(n, PU, stride=NI), :]
        left_scr[PU:, lanes] = rows_scr[1, pl.ds(n, PU, stride=NI), :]
    field = left_wide(pl_ref, left_scr[...])
    field_ref[...] = field
    intensity = field[:PP] * field[:PP] + field[PP:] * field[PP:]
    sums = jnp.concatenate(
        [jnp.sum(intensity[:, n * LANES : (n + 1) * LANES], axis=0, keepdims=True) for n in range(NI)], axis=0
    )
    scale = 1.0 / jnp.sum(sums, axis=1, keepdims=True)
    scale_ref[...] = jnp.broadcast_to(scale, (NI, LANES))
    spread = jnp.concatenate(
        [intensity[:, n * LANES : (n + 1) * LANES] * scale[n : n + 1, :] for n in range(NI)], axis=1
    )
    pair = jnp.concatenate([spread[:, : PC * LANES], spread[:, PC * LANES :]], axis=0)
    spec_ref[...] = right(to_rows(left(fl_ref, pair)), fr_ref)


def misfit_kernel(offsets_ref, kinds_ref, counts_ref, object_ref, data_ref, on_ref, off_ref, spec_ref, windows_ref,
                  rl_ref, fl_ref, fr_ref, ir_ref, il_ref, gl_ref,
                  obj_spec_ref, res_spec_ref, centre_ref, on_rim_ref, off_rim_ref, ext, total):
    even = lax.axis_index("patch") % 2 == 0
    on_at = pl.multiple_of(jnp.where(even, STRIDE + HALO, 0), 8)
    off_at = pl.multiple_of(jnp.where(even, 0, STRIDE + HALO), 8)
    edge = jnp.zeros((HEIGHT, LANES), F32)
    mid = slice(LANES, 3 * LANES)
    for i in range(1 + FK):
        ext[i, :, 0:LANES] = edge
        ext[i, :, 3 * LANES :] = edge
        ext[i, STRIDE + 2 * HALO :, mid] = jnp.zeros((HEIGHT - STRIDE - 2 * HALO, 2 * LANES), F32)
        ext[i, HALO : HALO + STRIDE, mid] = object_ref[...] if i == 0 else data_ref[:, i - 1, :]
        ext[i, pl.ds(on_at, HALO), mid] = on_ref[i * HALO : (i + 1) * HALO, :]
        ext[i, pl.ds(off_at, HALO), mid] = off_ref[i * HALO : (i + 1) * HALO, :]

    row_base = [pl.multiple_of((offsets_ref[0, c, 0] >> 3) << 3, 8) for c in range(PC)]
    row_rest = [offsets_ref[0, c, 0] & 7 for c in range(PC)]
    base = [0, LANES, LANES, 2 * LANES]
    shift = [LANES + c * STRIDE - HALO - base[c] + offsets_ref[0, c, 1] for c in range(PC)]

    def cut(i, c):
        block = ext[i, pl.ds(row_base[c], TALL), base[c] : base[c] + 2 * LANES]
        moved = pltpu.roll(block, 2 * LANES - shift[c], 1)[:, :LANES]
        return pltpu.roll(moved, jnp.where(row_rest[c] == 0, 0, TALL - row_rest[c]), 0)[:PP]

    windows = [windows_ref[kinds_ref[0, c]] for c in range(PC)]
    weighted = jnp.concatenate([windows[c] * cut(0, c) for c in range(PC)], axis=1)
    obj = right(to_rows(left_wide(rl_ref, weighted)), fr_ref)
    obj_spec_ref[...] = obj
    spec = spec_ref[...]
    o_re, o_im, s_re, s_im = obj[:, :LANES], obj[:, LANES:], spec[:, :LANES], spec[:, LANES:]
    product = jnp.concatenate([o_re * s_re - o_im * s_im, o_re * s_im + o_im * s_re], axis=1)
    predicted = left(il_ref, to_lanes(right(product, ir_ref)))
    parts = []
    for k in range(FK):
        for c in range(PC):
            usable = jnp.where(c < counts_ref[0], 1.0, 0.0).astype(F32)
            lanes = slice(c * LANES, (c + 1) * LANES)
            here = predicted[k * PP : (k + 1) * PP, lanes] * (1.0 / (PP * PP))
            parts.append((here - windows[c] * cut(k + 1, c)) * usable)
    residual = jnp.concatenate([jnp.concatenate(parts[k * PC : (k + 1) * PC], axis=1) for k in range(FK)], axis=0)
    res = right(to_rows(left(fl_ref, residual)), fr_ref)
    res_spec_ref[...] = res
    r_re, r_im = res[:, :LANES], res[:, LANES:]
    back = jnp.concatenate([s_re * r_re + s_im * r_im, s_re * r_im - s_im * r_re], axis=1)
    grad = left(gl_ref, to_lanes(right(back, ir_ref)))
    total[...] = jnp.zeros_like(total)
    for c in range(PC):
        mine = windows[c] * grad[:, c * LANES : (c + 1) * LANES] * (1.0 / (PP * PP))
        mine = pltpu.roll(jnp.concatenate([mine, jnp.zeros((TALL - PP, LANES), F32)], axis=0), row_rest[c], 0)
        placed = pltpu.roll(jnp.concatenate([mine, jnp.zeros((TALL, LANES), F32)], axis=1), shift[c], 1)
        rows, lanes = pl.ds(row_base[c], TALL), slice(base[c], base[c] + 2 * LANES)
        total[rows, lanes] = total[rows, lanes] + placed
    centre_ref[...] = total[HALO : HALO + STRIDE, mid]
    on_rim_ref[...] = total[pl.ds(on_at, HALO), mid]
    off_rim_ref[...] = total[pl.ds(off_at, HALO), mid]


def mode_kernel(obj_spec_ref, res_spec_ref, field_ref, scale_ref, pupil_ref, basis_ref, ir_ref, il_ref, bl_ref, br_ref,
                out_ref, rows_scr, flat_scr):
    obj, res = obj_spec_ref[...], res_spec_ref[...]
    o_re, o_im, r_re, r_im = obj[:, :LANES], obj[:, LANES:], res[:, :LANES], res[:, LANES:]
    back = jnp.concatenate([o_re * r_re + o_im * r_im, o_re * r_im - o_im * r_re], axis=1)
    grad = left(il_ref, to_lanes(right(back, ir_ref)))
    re_parts, im_parts = [], []
    for n in range(NI):
        k, c = divmod(n, PC)
        lanes = slice(n * LANES, (n + 1) * LANES)
        f_re, f_im = field_ref[:PP, lanes], field_ref[PP:, lanes]
        scale = scale_ref[n : n + 1, :]
        spread = (f_re * f_re + f_im * f_im) * scale
        mine = grad[k * PP : (k + 1) * PP, c * LANES : (c + 1) * LANES] * (1.0 / (PP * PP))
        mean = jnp.sum(jnp.sum(mine * spread, axis=0, keepdims=True), axis=1, keepdims=True)
        slope = 2.0 * scale * (mine - mean)
        re_parts.append(f_re * slope)
        im_parts.append(f_im * slope)
    wide = jnp.concatenate([jnp.concatenate(re_parts, axis=1), jnp.concatenate(im_parts, axis=1)], axis=0)
    half = left(bl_ref, wide)
    for n in range(NI):
        lanes = slice(n * LANES, (n + 1) * LANES)
        rows_scr[0, pl.ds(n, PU, stride=NI), :] = half[:PU, lanes]
        rows_scr[1, pl.ds(n, PU, stride=NI), :] = half[PU:, lanes]
    pupil_grad = right(jnp.concatenate([rows_scr[0], rows_scr[1]], axis=1), br_ref)
    pupil = pupil_ref[...]
    crossed = pupil * pltpu.roll(pupil_grad, 64, 1)
    slopes = crossed - pltpu.roll(crossed, 64, 1)
    for a in range(PU):
        flat_scr[:, a * PU : (a + 1) * PU] = slopes[a * NI : (a + 1) * NI, 0:PU]
    high, low = split(flat_scr[...])
    b_high, b_low = split(basis_ref[...])

    def by_modes(a, b):
        return lax.dot_general(a, b, (((1,), (1,)), ((), ())), preferred_element_type=F32)

    both = by_modes(jnp.concatenate([high, low], axis=0), b_high)
    out = both[:NI] + both[NI:] + by_modes(high, b_low)
    out_ref[0, 0] = out[:PC]
    out_ref[1, 0] = out[PC:]


def call(kernel, out_shapes, scratch=(), smem=0, inputs=0, name=None):
    vmem = pl.BlockSpec(memory_space=pltpu.VMEM)
    return pl.pallas_call(
        kernel,
        out_shape=out_shapes,
        in_specs=[pl.BlockSpec(memory_space=pltpu.SMEM)] * smem + [vmem] * inputs,
        out_specs=jax.tree.map(lambda _: vmem, out_shapes),
        scratch_shapes=list(scratch),
        compiler_params=pltpu.CompilerParams(vmem_limit_bytes=VMEM_LIMIT),
        name=name,
    )


def shape(*dims):
    return jax.ShapeDtypeStruct(dims, F32)


def swap_on(values):
    count = lax.axis_size("patch")
    return lax.ppermute(values, "patch", [(i, i ^ 1) for i in range(count)])


def swap_off(values):
    count = lax.axis_size("patch")
    pairs = [(i, i + 1) for i in range(1, count - 1, 2)]
    return lax.ppermute(values, "patch", pairs + [(j, i) for i, j in pairs])


def swap_frames(values, bit):
    count = lax.axis_size("frames")
    return lax.ppermute(values, "frames", [(i, i ^ bit) for i in range(count)])


def body(object_band, data_band, coeffs, mode_basis, offsets, window_ids, counts):
    columns = object_band.shape[1]
    const = {name: jnp.asarray(value) for name, value in constants().items()}
    on_send, off_send = call(pack_kernel, [shape(3 * HALO, columns)] * 2, inputs=2, name="pack")(object_band, data_band)
    off_halo = swap_off(off_send)
    on_halo = swap_on(on_send)
    pupil, field, spec, scale = call(
        psf_kernel,
        [shape(PU * NI, LANES), shape(2 * PP, NI * LANES), shape(PC * PP, 2 * LANES), shape(NI, LANES)],
        scratch=[pltpu.VMEM((2, PU * NI, LANES), F32), pltpu.VMEM((2 * PU, NI * LANES), F32)],
        inputs=7,
        name="psf",
    )(coeffs, mode_basis, const["opening"], const["pupil_right"], const["pupil_left"], const["fwd_left"], const["fwd_right"])
    obj_spec, res_spec, centre, on_rim, off_rim = call(
        misfit_kernel,
        [shape(PC * PP, 2 * LANES)] * 2 + [shape(STRIDE, columns), shape(HALO, columns), shape(HALO, columns)],
        scratch=[pltpu.VMEM((1 + FK, HEIGHT, 4 * LANES), F32), pltpu.VMEM((HEIGHT, 4 * LANES), F32)],
        smem=3,
        inputs=12,
        name="misfit",
    )(
        offsets, window_ids, counts, object_band, data_band, on_halo, off_halo, spec, const["windows"],
        const["real_left"], const["fwd_left"], const["fwd_right"], const["inv_right"], const["inv_left"], const["part_left"],
    )
    on_rim = swap_on(on_rim)
    off_rim = swap_off(off_rim)
    even = lax.axis_index("patch") % 2 == 0
    upper = jnp.where(even, off_rim, on_rim)
    lower = jnp.where(even, on_rim, off_rim)
    rows = jnp.concatenate([centre[:HALO] + upper, centre[HALO : STRIDE - HALO], centre[STRIDE - HALO :] + lower], axis=0)
    for bit in (4, 1, 2):
        rows = rows + swap_frames(rows, bit)
    coeff_grad = call(
        mode_kernel,
        shape(FK, 1, PC, MODES),
        scratch=[pltpu.VMEM((2, PU * NI, LANES), F32), pltpu.VMEM((NI, PU * PU), F32)],
        inputs=10,
        name="modes",
    )(
        obj_spec, res_spec, field, scale, pupil, mode_basis,
        const["inv_right"], const["inv_left"], const["back_left"], const["back_right"],
    )
    return rows, coeff_grad


def solution(mesh):
    in_specs = (
        P("patch", None),
        P("patch", "frames", None),
        P("frames", "patch", None, None),
        P(),
        P("patch", None, None),
        P("patch", None),
        P("patch"),
    )
    out_specs = (P("patch", None), P("frames", "patch", None, None))
    return jax.shard_map(body, mesh=mesh, in_specs=in_specs, out_specs=out_specs, check_vma=False)
```

```python
import math

import jax
import jax.numpy as jnp
import ml_dtypes
import numpy as np
from jax import lax
from jax.experimental import pallas as pl
from jax.experimental.pallas import tpu as pltpu
from jax.sharding import PartitionSpec as P

PP = 96
PU = 48
STRIDE = 64
HALO = 24
PC = 4
FK = 2
NI = PC * FK
LANES = 128
MODES = 200
TALL = PP + 8
HEIGHT = STRIDE + 2 * HALO + 8
F32 = jnp.float32
BF16 = jnp.bfloat16
VMEM_LIMIT = 8 * 1024 * 1024
CHUNK = 768
CHUNKS = PU * PU // CHUNK


def halves(matrix):
    high = matrix.astype(ml_dtypes.bfloat16)
    low = (matrix - high.astype(np.float64)).astype(ml_dtypes.bfloat16)
    return high, low


def dft(points, length):
    turns = np.outer(np.arange(points), np.arange(length)) % points
    angles = 2.0 * math.pi / points * turns
    return np.cos(angles), -np.sin(angles)


def constants():
    full_re, full_im = dft(PP, PP)
    half_re, half_im = dft(PP, PU)
    fwd_right = np.zeros((256, 256))
    fwd_right[:96, :96] = full_re
    fwd_right[128:224, :96] = -full_im
    fwd_right[:96, 128:224] = full_im
    fwd_right[128:224, 128:224] = full_re
    pupil_right = np.zeros((128, 256))
    pupil_right[:48, :96] = half_re.T
    pupil_right[64:112, :96] = -half_im.T
    pupil_right[:48, 128:224] = half_im.T
    pupil_right[64:112, 128:224] = half_re.T
    pupil_left = np.block([[half_re, -half_im], [half_im, half_re]])
    fwd_left = np.block([[full_re, -full_im], [full_im, full_re]])
    real_left = np.concatenate([full_re, full_im], axis=0)

    def stack(matrix):
        return np.concatenate(halves(matrix), axis=0)

    def twice(matrix):
        high, low = halves(matrix)
        return np.concatenate([high, low], axis=1)

    side = np.arange(PP) + 0.5
    windows = np.zeros((4, PP, LANES), np.float32)
    for kind in range(4):
        edge = float(max(PP * (kind + 1) // 12, 1))
        rising = 0.5 - 0.5 * np.cos(math.pi * np.minimum(side, edge) / edge)
        profile = rising * rising[::-1]
        windows[kind, :, :PP] = np.outer(profile, profile)
    centre = np.arange(PU) + 0.5 - 0.5 * PU
    opening = (centre[:, None] ** 2 + centre[None, :] ** 2 <= (0.5 * PU) ** 2).reshape(1, PU * PU)
    return {
        "fwd_right": stack(fwd_right),
        "pupil_right": stack(pupil_right),
        "pupil_left": twice(pupil_left),
        "fwd_left": stack(fwd_left),
        "real_left": twice(real_left),
        "back_left": stack(pupil_left.T.copy()),
        "back_right": stack(pupil_right.T.copy()),
        "windows": windows,
        "opening": opening.astype(np.float32),
    }


def split(values):
    high = values.astype(BF16)
    return high, (values - high.astype(F32)).astype(BF16)


def mm(a, b):
    return jnp.dot(a, b, preferred_element_type=F32)


def right(values, matrix_ref):
    depth = matrix_ref.shape[0] // 2
    rows = values.shape[0]
    high, low = split(values)
    both = mm(jnp.concatenate([high, low], axis=0), matrix_ref[:depth])
    return both[:rows] + both[rows:] + mm(high, matrix_ref[depth:])


def left(matrix_ref, values):
    rows = matrix_ref.shape[0] // 2
    high, low = split(values)
    both = mm(matrix_ref[...], high)
    return both[:rows] + both[rows:] + mm(matrix_ref[:rows], low)


def left_part(matrix_ref, values):
    rows = matrix_ref.shape[0] // 2
    half = rows // 2
    high, low = split(values)
    return mm(matrix_ref[:half], high) + mm(matrix_ref[rows : rows + half], high) + mm(matrix_ref[:half], low)


def left_wide(matrix_ref, values):
    depth = values.shape[0]
    high, low = split(values)
    return mm(matrix_ref[...], jnp.concatenate([high, high], axis=0)) + mm(matrix_ref[:, :depth], low)


def to_rows(spectrum):
    parts = []
    for c in range(PC):
        lanes = slice(c * LANES, (c + 1) * LANES)
        parts.append(jnp.concatenate([spectrum[:PP, lanes], spectrum[PP:, lanes]], axis=1))
    return jnp.concatenate(parts, axis=0)


def to_lanes(rows):
    re = jnp.concatenate([rows[c * PP : (c + 1) * PP, :LANES] for c in range(PC)], axis=1)
    im = jnp.concatenate([rows[c * PP : (c + 1) * PP, LANES:] for c in range(PC)], axis=1)
    return jnp.concatenate([re, im], axis=0)


def sin_cos(angle):
    turns = jnp.floor(angle * (2.0 / math.pi) + 0.5)
    rest = angle - turns * 1.5703125
    rest = rest - turns * 4.837512969970703125e-4
    rest = rest - turns * 7.54978995489188216e-8
    sq = rest * rest
    sine = ((-1.9515295891e-4 * sq + 8.3321608736e-3) * sq - 1.6666654611e-1) * sq * rest + rest
    cosine = ((2.443315711809948e-5 * sq - 1.388731625493765e-3) * sq + 4.166664568298827e-2) * sq * sq - 0.5 * sq + 1.0
    quarter = turns.astype(jnp.int32) & 3
    swapped = (quarter & 1) == 1
    sin_now = jnp.where(swapped, cosine, sine)
    cos_now = jnp.where(swapped, sine, cosine)
    sin_now = jnp.where(quarter >= 2, -sin_now, sin_now)
    cos_now = jnp.where((quarter == 1) | (quarter == 2), -cos_now, cos_now)
    return sin_now, cos_now


def fetch(pairs, sems):
    copies = [pltpu.make_async_copy(src, dst, sems.at[i]) for i, (src, dst) in enumerate(pairs)]
    for copy in copies:
        copy.start()
    return copies


def pack_kernel(object_hbm, data_hbm, on_ref, off_ref, on_scr, off_scr, sems):
    even = lax.axis_index("patch") % 2 == 0
    low, high = STRIDE - HALO, 0
    on_at = pl.multiple_of(jnp.where(even, low, high), 8)
    off_at = pl.multiple_of(jnp.where(even, high, low), 8)
    copies = fetch(
        [
            (object_hbm.at[pl.ds(off_at, HALO)], off_ref.at[pl.ds(0, HALO)]),
            (data_hbm.at[pl.ds(off_at, HALO)], off_scr),
            (object_hbm.at[pl.ds(on_at, HALO)], on_ref.at[pl.ds(0, HALO)]),
            (data_hbm.at[pl.ds(on_at, HALO)], on_scr),
        ],
        sems,
    )
    for copy in copies:
        copy.wait()
    for k in range(FK):
        rows = slice((k + 1) * HALO, (k + 2) * HALO)
        off_ref[rows, :] = off_scr[:, k, :]
        on_ref[rows, :] = on_scr[:, k, :]


def psf_kernel(coeffs_hbm, object_hbm, data_hbm, opening_hbm, basis_hbm, pr_hbm, pl_hbm, fl_hbm, fr_hbm,
               windows_hbm, rl_hbm, bl_hbm, br_hbm,
               pupil_ref, field_ref, spec_ref, scale_ref, ext, fl_ref, fr_ref,
               windows_ref, rl_ref, bl_ref, br_ref,
               basis_scr, wave_scr, rows_scr, left_scr, coeffs_ref, data_scr, opening_ref, pr_ref, pl_ref, sems):
    chunks = [(basis_hbm.at[:, pl.ds(j * CHUNK, CHUNK)], basis_scr.at[j]) for j in range(CHUNKS)]
    copies = fetch(
        [
            (coeffs_hbm, coeffs_ref),
            (object_hbm, ext.at[0, pl.ds(HALO, STRIDE), pl.ds(LANES, 2 * LANES)]),
            (data_hbm, data_scr),
        ] + chunks + [
            (opening_hbm, opening_ref), (pr_hbm, pr_ref), (pl_hbm, pl_ref), (fl_hbm, fl_ref), (fr_hbm, fr_ref),
            (windows_hbm, windows_ref), (rl_hbm, rl_ref), (bl_hbm, bl_ref), (br_hbm, br_ref),
        ],
        sems,
    )
    for i in range(1 + FK):
        ext[i, :, 0:LANES] = jnp.zeros((HEIGHT, LANES), F32)
        ext[i, :, 3 * LANES :] = jnp.zeros((HEIGHT, LANES), F32)
        ext[i, STRIDE + 2 * HALO :, LANES : 3 * LANES] = jnp.zeros((HEIGHT - STRIDE - 2 * HALO, 2 * LANES), F32)
    pupil_ref[...] = jnp.zeros_like(pupil_ref)
    copies[0].wait()
    copies[1].wait()
    copies[2].wait()
    for k in range(FK):
        ext[k + 1, HALO : HALO + STRIDE, LANES : 3 * LANES] = data_scr[:, k, :]
    copies = copies[3:]
    coeffs = jnp.concatenate([coeffs_ref[0, 0], coeffs_ref[1, 0]], axis=0)
    c_high = coeffs.astype(BF16)
    rest = coeffs - c_high.astype(F32)
    c_mid = rest.astype(BF16)
    c_low = (rest - c_mid.astype(F32)).astype(BF16)
    c_all = jnp.concatenate([c_high, c_mid, c_low], axis=0)
    for j in range(CHUNKS):
        copies[j].wait()
        basis = basis_scr[j]
        b_high = basis.astype(BF16)
        b_rest = basis - b_high.astype(F32)
        b_mid = b_rest.astype(BF16)
        b_low = (b_rest - b_mid.astype(F32)).astype(BF16)
        by_high, by_mid, by_low = mm(c_all, b_high), mm(c_all[: 2 * NI], b_mid), mm(c_high, b_low)
        small = by_low + by_mid[NI:] + by_high[2 * NI :]
        wave_scr[:, j * CHUNK : (j + 1) * CHUNK] = small + (by_mid[:NI] + by_high[NI : 2 * NI]) + by_high[:NI]
    wave = wave_scr[...]
    sine, cosine = sin_cos(wave)
    copies[CHUNKS].wait()
    opening = opening_ref[...]
    re = cosine * opening
    im = sine * opening
    for a in range(PU):
        pupil_ref[a * NI : (a + 1) * NI, 0:PU] = re[:, a * PU : (a + 1) * PU]
        pupil_ref[a * NI : (a + 1) * NI, 64 : 64 + PU] = im[:, a * PU : (a + 1) * PU]
    copies[CHUNKS + 1].wait()
    mixed = right(pupil_ref[...], pr_ref)
    rows_scr[0] = mixed[:, :LANES]
    rows_scr[1] = mixed[:, LANES:]
    for n in range(NI):
        lanes = slice(n * LANES, (n + 1) * LANES)
        left_scr[0:PU, lanes] = rows_scr[0, pl.ds(n, PU, stride=NI), :]
        left_scr[PU:, lanes] = rows_scr[1, pl.ds(n, PU, stride=NI), :]
    copies[CHUNKS + 2].wait()
    field = left_wide(pl_ref, left_scr[...])
    field_ref[...] = field
    intensity = field[:PP] * field[:PP] + field[PP:] * field[PP:]
    sums = jnp.concatenate(
        [jnp.sum(intensity[:, n * LANES : (n + 1) * LANES], axis=0, keepdims=True) for n in range(NI)], axis=0
    )
    scale = 1.0 / jnp.sum(sums, axis=1, keepdims=True)
    scale_ref[...] = jnp.broadcast_to(scale, (NI, LANES))
    spread = jnp.concatenate(
        [intensity[:, n * LANES : (n + 1) * LANES] * scale[n : n + 1, :] for n in range(NI)], axis=1
    )
    pair = jnp.concatenate([spread[:, : PC * LANES], spread[:, PC * LANES :]], axis=0)
    copies[CHUNKS + 3].wait()
    copies[CHUNKS + 4].wait()
    spec_ref[...] = right(to_rows(left(fl_ref, pair)), fr_ref)
    for copy in copies[CHUNKS + 5 :]:
        copy.wait()


def misfit_kernel(offsets_ref, kinds_ref, counts_ref, on_ref, off_ref, spec_ref, ext_in, windows_ref, rl_ref, fl_ref, fr_ref,
                  obj_spec_ref, res_spec_ref, centre_ref, on_rim_ref, off_rim_ref, ext, total):
    even = lax.axis_index("patch") % 2 == 0
    on_at = pl.multiple_of(jnp.where(even, STRIDE + HALO, 0), 8)
    off_at = pl.multiple_of(jnp.where(even, 0, STRIDE + HALO), 8)
    mid = slice(LANES, 3 * LANES)
    total[...] = jnp.zeros_like(total)
    for i in range(1 + FK):
        ext[i] = ext_in[i]
        ext[i, pl.ds(on_at, HALO), mid] = on_ref[i * HALO : (i + 1) * HALO, :]
        ext[i, pl.ds(off_at, HALO), mid] = off_ref[i * HALO : (i + 1) * HALO, :]

    row_base = [pl.multiple_of((offsets_ref[0, 0, c] >> 3) << 3, 8) for c in range(PC)]
    row_rest = [offsets_ref[0, 0, c] & 7 for c in range(PC)]
    base = [0, LANES, LANES, 2 * LANES]
    shift = [LANES + c * STRIDE - HALO - base[c] + offsets_ref[0, 1, c] for c in range(PC)]

    def cut(i, c):
        block = ext[i, pl.ds(row_base[c], TALL), base[c] : base[c] + 2 * LANES]
        moved = pltpu.roll(block, 2 * LANES - shift[c], 1)[:, :LANES]
        return pltpu.roll(moved, jnp.where(row_rest[c] == 0, 0, TALL - row_rest[c]), 0)[:PP]

    windows = [windows_ref[kinds_ref[0, c]] for c in range(PC)]
    weighted = jnp.concatenate([windows[c] * cut(0, c) for c in range(PC)], axis=1)
    obj = right(to_rows(left_wide(rl_ref, weighted)), fr_ref)
    obj_spec_ref[...] = obj
    spec = spec_ref[...]
    o_re, o_im, s_re, s_im = obj[:, :LANES], obj[:, LANES:], spec[:, :LANES], spec[:, LANES:]
    product = jnp.concatenate([o_re * s_re - o_im * s_im, -(o_re * s_im + o_im * s_re)], axis=1)
    predicted = left(fl_ref, to_lanes(right(product, fr_ref)))
    parts = []
    for k in range(FK):
        for c in range(PC):
            usable = jnp.where(c < counts_ref[0], 1.0, 0.0).astype(F32)
            lanes = slice(c * LANES, (c + 1) * LANES)
            here = predicted[k * PP : (k + 1) * PP, lanes] * ((1 - 2 * k) / (PP * PP))
            parts.append((here - windows[c] * cut(k + 1, c)) * usable)
    residual = jnp.concatenate([jnp.concatenate(parts[k * PC : (k + 1) * PC], axis=1) for k in range(FK)], axis=0)
    res = right(to_rows(left(fl_ref, residual)), fr_ref)
    res_spec_ref[...] = res
    r_re, r_im = res[:, :LANES], res[:, LANES:]
    back = jnp.concatenate([s_re * r_re + s_im * r_im, s_im * r_re - s_re * r_im], axis=1)
    grad = left_part(fl_ref, to_lanes(right(back, fr_ref)))
    for c in range(PC):
        mine = windows[c] * grad[:, c * LANES : (c + 1) * LANES] * (1.0 / (PP * PP))
        mine = pltpu.roll(jnp.concatenate([mine, jnp.zeros((TALL - PP, LANES), F32)], axis=0), row_rest[c], 0)
        placed = pltpu.roll(jnp.concatenate([mine, jnp.zeros((TALL, LANES), F32)], axis=1), shift[c], 1)
        rows, lanes = pl.ds(row_base[c], TALL), slice(base[c], base[c] + 2 * LANES)
        total[rows, lanes] = total[rows, lanes] + placed
    centre_ref[...] = total[HALO : HALO + STRIDE, mid]
    on_rim_ref[...] = total[pl.ds(on_at, HALO), mid]
    off_rim_ref[...] = total[pl.ds(off_at, HALO), mid]


def spread_grad_kernel(obj_spec_ref, res_spec_ref, fl_ref, fr_ref, grad_ref):
    obj, res = obj_spec_ref[...], res_spec_ref[...]
    o_re, o_im, r_re, r_im = obj[:, :LANES], obj[:, LANES:], res[:, :LANES], res[:, LANES:]
    back = jnp.concatenate([o_re * r_re + o_im * r_im, o_im * r_re - o_re * r_im], axis=1)
    grad_ref[...] = left(fl_ref, to_lanes(right(back, fr_ref)))


def mode_kernel(grad_ref, field_ref, scale_ref, pupil_ref, bl_ref, br_ref, basis_hbm, out_ref, rows_scr, flat_ref, basis_scr, sems):
    copies = fetch([(basis_hbm.at[:, pl.ds(j * CHUNK, CHUNK)], basis_scr.at[j]) for j in range(CHUNKS)], sems)
    re_parts, im_parts = [], []
    for n in range(NI):
        k, c = divmod(n, PC)
        lanes = slice(n * LANES, (n + 1) * LANES)
        f_re, f_im = field_ref[:PP, lanes], field_ref[PP:, lanes]
        scale = scale_ref[n : n + 1, :]
        spread = (f_re * f_re + f_im * f_im) * scale
        mine = grad_ref[k * PP : (k + 1) * PP, c * LANES : (c + 1) * LANES] * ((1 - 2 * k) / (PP * PP))
        mean = jnp.sum(jnp.sum(mine * spread, axis=0, keepdims=True), axis=1, keepdims=True)
        slope = 2.0 * scale * (mine - mean)
        re_parts.append(f_re * slope)
        im_parts.append(f_im * slope)
    wide = jnp.concatenate([jnp.concatenate(re_parts, axis=1), jnp.concatenate(im_parts, axis=1)], axis=0)
    half = left(bl_ref, wide)
    for n in range(NI):
        lanes = slice(n * LANES, (n + 1) * LANES)
        rows_scr[0, pl.ds(n, PU, stride=NI), :] = half[:PU, lanes]
        rows_scr[1, pl.ds(n, PU, stride=NI), :] = half[PU:, lanes]
    pupil_grad = right(jnp.concatenate([rows_scr[0], rows_scr[1]], axis=1), br_ref)
    pupil = pupil_ref[...]
    crossed = pupil * pltpu.roll(pupil_grad, 64, 1)
    slopes = crossed - pltpu.roll(crossed, 64, 1)
    for a in range(PU):
        flat_ref[:, a * PU : (a + 1) * PU] = slopes[a * NI : (a + 1) * NI, 0:PU]
    flat_high, flat_low = split(flat_ref[...])
    both = jnp.concatenate([flat_high, flat_low], axis=0)

    def by_modes(a, b):
        return lax.dot_general(a, b, (((1,), (1,)), ((), ())), preferred_element_type=F32)

    out = jnp.zeros((NI, MODES), F32)
    for j in range(CHUNKS):
        copies[j].wait()
        b_high, b_low = split(basis_scr[j])
        lanes = slice(j * CHUNK, (j + 1) * CHUNK)
        first = by_modes(both[:, lanes], b_high)
        out = out + (first[:NI] + first[NI:] + by_modes(flat_high[:, lanes], b_low))
    out_ref[0, 0] = out[:PC]
    out_ref[1, 0] = out[PC:]


def call(kernel, out_shapes, scratch=(), smem=0, near=0, far=0, name=None):
    vmem = pl.BlockSpec(memory_space=pltpu.VMEM)
    inner = pl.pallas_call(
        kernel,
        out_shape=out_shapes,
        in_specs=[pl.BlockSpec(memory_space=pltpu.SMEM)] * smem + [vmem] * near + [pl.BlockSpec(memory_space=pltpu.HBM)] * far,
        out_specs=jax.tree.map(lambda _: vmem, out_shapes),
        scratch_shapes=list(scratch),
        compiler_params=pltpu.CompilerParams(vmem_limit_bytes=VMEM_LIMIT),
        name=name,
    )

    def run(*operands):
        placed = list(operands)
        for i in range(smem + near, smem + near + far):
            placed[i] = pltpu.with_memory_space_constraint(placed[i], pltpu.HBM)
        for i in range(smem, smem + near):
            placed[i] = pltpu.with_memory_space_constraint(placed[i], pltpu.VMEM)
        return inner(*placed)

    return run


def shape(*dims):
    return pltpu.VMEM(dims, F32)


def sems(count):
    return pltpu.SemaphoreType.DMA((count,))


def like(value):
    return pltpu.VMEM(value.shape, BF16 if value.dtype == ml_dtypes.bfloat16 else F32)


def swap_on(values):
    count = lax.axis_size("patch")
    return lax.ppermute(values, "patch", [(i, i ^ 1) for i in range(count)])


def swap_off(values):
    count = lax.axis_size("patch")
    pairs = [(i, i + 1) for i in range(1, count - 1, 2)]
    return lax.ppermute(values, "patch", pairs + [(j, i) for i, j in pairs])


def swap_frames(values, bit):
    count = lax.axis_size("frames")
    return lax.ppermute(values, "frames", [(i, i ^ bit) for i in range(count)])


def body(object_band, data_band, coeffs, mode_basis, offsets, window_ids, counts):
    columns = object_band.shape[1]
    host = constants()
    const = {name: jnp.asarray(value) for name, value in host.items()}
    room = {name: like(value) for name, value in host.items()}
    halo_room = pltpu.VMEM((HALO, FK, columns), F32)
    on_send, off_send = call(
        pack_kernel, [shape(3 * HALO, columns)] * 2, scratch=[halo_room, halo_room, sems(4)], far=2, name="pack",
    )(object_band, data_band)
    off_halo = swap_off(off_send)
    on_halo = swap_on(on_send)
    given = ("opening", "pupil_right", "pupil_left", "fwd_left", "fwd_right", "windows", "real_left", "back_left", "back_right")
    kept = ("fwd_left", "fwd_right", "windows", "real_left", "back_left", "back_right")
    pupil, field, spec, scale, ext, *kept_values = call(
        psf_kernel,
        [shape(PU * NI, LANES), shape(2 * PP, NI * LANES), shape(PC * PP, 2 * LANES), shape(NI, LANES),
         shape(1 + FK, HEIGHT, 4 * LANES)] + [room[name] for name in kept],
        scratch=[
            pltpu.VMEM((CHUNKS, MODES, CHUNK), F32), pltpu.VMEM((NI, PU * PU), F32), pltpu.VMEM((2, PU * NI, LANES), F32),
            pltpu.VMEM((2 * PU, NI * LANES), F32), pltpu.VMEM((FK, 1, PC, MODES), F32), pltpu.VMEM((STRIDE, FK, columns), F32),
            room["opening"], room["pupil_right"], room["pupil_left"], sems(CHUNKS + 12),
        ],
        far=13,
        name="psf",
    )(coeffs, object_band, data_band, const["opening"], mode_basis, *[const[name] for name in given[1:]])
    here = dict(zip(kept, kept_values))
    obj_spec, res_spec, centre, on_rim, off_rim = call(
        misfit_kernel,
        [shape(PC * PP, 2 * LANES)] * 2 + [shape(STRIDE, columns), shape(HALO, columns), shape(HALO, columns)],
        scratch=[pltpu.VMEM((1 + FK, HEIGHT, 4 * LANES), F32), pltpu.VMEM((HEIGHT, 4 * LANES), F32)],
        smem=3,
        near=8,
        name="misfit",
    )(
        jnp.transpose(offsets, (0, 2, 1)), window_ids, counts, on_halo, off_halo, spec, ext,
        here["windows"], here["real_left"], here["fwd_left"], here["fwd_right"],
    )
    on_rim = swap_on(on_rim)
    off_rim = swap_off(off_rim)
    spread_grad = call(spread_grad_kernel, shape(2 * PP, PC * LANES), near=4, name="spread_grad")(
        obj_spec, res_spec, here["fwd_left"], here["fwd_right"]
    )
    even = lax.axis_index("patch") % 2 == 0
    upper = jnp.where(even, off_rim, on_rim)
    lower = jnp.where(even, on_rim, off_rim)
    rows = jnp.concatenate([centre[:HALO] + upper, centre[HALO : STRIDE - HALO], centre[STRIDE - HALO :] + lower], axis=0)
    rows, spread_grad = lax.optimization_barrier((rows, spread_grad))
    moved = swap_frames(rows, 4)
    coeff_grad = call(
        mode_kernel, jax.ShapeDtypeStruct((FK, 1, PC, MODES), F32),
        scratch=[
            pltpu.VMEM((2, PU * NI, LANES), F32), pltpu.VMEM((NI, PU * PU), F32), pltpu.VMEM((CHUNKS, MODES, CHUNK), F32), sems(CHUNKS),
        ],
        near=6, far=1, name="modes",
    )(spread_grad, field, scale, pupil, here["back_left"], here["back_right"], mode_basis)
    rows = rows + moved
    rows, coeff_grad = lax.optimization_barrier((rows, coeff_grad))
    rows = rows + swap_frames(rows, 1)
    rows = rows + swap_frames(rows, 2)
    return rows, coeff_grad


def solution(mesh):
    in_specs = (
        P("patch", None),
        P("patch", "frames", None),
        P("frames", "patch", None, None),
        P(),
        P("patch", None, None),
        P("patch", None),
        P("patch"),
    )
    out_specs = (P("patch", None), P("frames", "patch", None, None))
    return jax.shard_map(body, mesh=mesh, in_specs=in_specs, out_specs=out_specs, check_vma=False)
```

```python
import math

import jax
import jax.numpy as jnp
import ml_dtypes
import numpy as np
from jax import lax
from jax.experimental import pallas as pl
from jax.experimental.pallas import tpu as pltpu
from jax.sharding import PartitionSpec as P

PP = 96
PU = 48
STRIDE = 64
HALO = 24
PC = 4
FK = 2
NI = PC * FK
LANES = 128
MODES = 200
TALL = PP + 8
HEIGHT = STRIDE + 2 * HALO + 8
F32 = jnp.float32
BF16 = jnp.bfloat16
VMEM_LIMIT = 16 * 1024 * 1024
CHUNK = 768
CHUNKS = PU * PU // CHUNK


def halves(matrix):
    high = matrix.astype(ml_dtypes.bfloat16)
    low = (matrix - high.astype(np.float64)).astype(ml_dtypes.bfloat16)
    return high, low


def dft(points, length):
    turns = np.outer(np.arange(points), np.arange(length)) % points
    angles = 2.0 * math.pi / points * turns
    return np.cos(angles), -np.sin(angles)


def constants():
    full_re, full_im = dft(PP, PP)
    half_re, half_im = dft(PP, PU)
    fwd_right = np.zeros((256, 256))
    fwd_right[:96, :96] = full_re
    fwd_right[128:224, :96] = -full_im
    fwd_right[:96, 128:224] = full_im
    fwd_right[128:224, 128:224] = full_re
    pupil_right = np.zeros((128, 256))
    pupil_right[:48, :96] = half_re.T
    pupil_right[64:112, :96] = -half_im.T
    pupil_right[:48, 128:224] = half_im.T
    pupil_right[64:112, 128:224] = half_re.T
    pupil_left = np.block([[half_re, -half_im], [half_im, half_re]])
    fwd_left = np.block([[full_re, -full_im], [full_im, full_re]])
    real_left = np.concatenate([full_re, full_im], axis=0)

    def tall(matrix):
        high, low = halves(matrix)
        return np.concatenate([high, low, high], axis=0)

    def wide(matrix):
        high, low = halves(matrix)
        return np.concatenate([high, low, high], axis=1)

    side = np.arange(PP) + 0.5
    windows = np.zeros((4, PP, LANES), np.float32)
    for kind in range(4):
        edge = float(max(PP * (kind + 1) // 12, 1))
        rising = 0.5 - 0.5 * np.cos(math.pi * np.minimum(side, edge) / edge)
        profile = rising * rising[::-1]
        windows[kind, :, :PP] = np.outer(profile, profile)
    centre = np.arange(PU) + 0.5 - 0.5 * PU
    opening = (centre[:, None] ** 2 + centre[None, :] ** 2 <= (0.5 * PU) ** 2).reshape(1, PU * PU)
    return {
        "fwd_right": tall(fwd_right),
        "pupil_right": tall(pupil_right),
        "pupil_left": wide(pupil_left),
        "fwd_left": wide(fwd_left),
        "real_left": wide(real_left),
        "back_left": wide(pupil_left.T),
        "back_right": tall(pupil_right.T),
        "windows": windows,
        "opening": opening.astype(np.float32),
    }


def split(values):
    high = values.astype(BF16)
    return high, (values - high.astype(F32)).astype(BF16)


def mm(a, b):
    return jnp.dot(a, b, preferred_element_type=F32)


def right(values, matrix):
    high, low = split(values)
    return mm(jnp.concatenate([high, high, low], axis=1), matrix[...])


def left(matrix, values):
    high, low = split(values)
    return mm(matrix[...], jnp.concatenate([high, high, low], axis=0))


def to_rows(spectrum):
    parts = []
    for c in range(PC):
        lanes = slice(c * LANES, (c + 1) * LANES)
        parts.append(jnp.concatenate([spectrum[:PP, lanes], spectrum[PP:, lanes]], axis=1))
    return jnp.concatenate(parts, axis=0)


def to_lanes(rows):
    re = jnp.concatenate([rows[c * PP : (c + 1) * PP, :LANES] for c in range(PC)], axis=1)
    im = jnp.concatenate([rows[c * PP : (c + 1) * PP, LANES:] for c in range(PC)], axis=1)
    return jnp.concatenate([re, im], axis=0)


def sin_cos(angle):
    turns = jnp.floor(angle * (2.0 / math.pi) + 0.5)
    rest = angle - turns * 1.5703125
    rest = rest - turns * 4.837512969970703125e-4
    rest = rest - turns * 7.54978995489188216e-8
    sq = rest * rest
    sine = ((-1.9515295891e-4 * sq + 8.3321608736e-3) * sq - 1.6666654611e-1) * sq * rest + rest
    cosine = ((2.443315711809948e-5 * sq - 1.388731625493765e-3) * sq + 4.166664568298827e-2) * sq * sq - 0.5 * sq + 1.0
    quarter = turns.astype(jnp.int32) & 3
    swapped = (quarter & 1) == 1
    sin_now = jnp.where(swapped, cosine, sine)
    cos_now = jnp.where(swapped, sine, cosine)
    sin_now = jnp.where(quarter >= 2, -sin_now, sin_now)
    cos_now = jnp.where((quarter == 1) | (quarter == 2), -cos_now, cos_now)
    return sin_now, cos_now


def fetch(pairs, sems):
    copies = [pltpu.make_async_copy(src, dst, sems.at[i]) for i, (src, dst) in enumerate(pairs)]
    for copy in copies:
        copy.start()
    return copies


def is_early():
    return lax.axis_index("patch") % 8 == 0


def pupil_part(coeffs_hbm, opening_hbm, basis_hbm, pupil_ref, basis_scr, wave_scr, coeffs_ref, opening_ref, sems):
    copies = fetch(
        [(coeffs_hbm, coeffs_ref)]
        + [(basis_hbm.at[:, pl.ds(j * CHUNK, CHUNK)], basis_scr.at[j]) for j in range(CHUNKS)]
        + [(opening_hbm, opening_ref)],
        sems,
    )
    pupil_ref[...] = jnp.zeros_like(pupil_ref)
    copies[0].wait()
    coeffs = jnp.concatenate([coeffs_ref[0, 0], coeffs_ref[1, 0]], axis=0)
    c_high = coeffs.astype(BF16)
    rest = coeffs - c_high.astype(F32)
    c_mid = rest.astype(BF16)
    c_low = (rest - c_mid.astype(F32)).astype(BF16)
    c_all = jnp.concatenate([c_high, c_mid, c_low], axis=0)
    for j in range(CHUNKS):
        copies[1 + j].wait()
        basis = basis_scr[j]
        b_high = basis.astype(BF16)
        b_rest = basis - b_high.astype(F32)
        b_mid = b_rest.astype(BF16)
        b_low = (b_rest - b_mid.astype(F32)).astype(BF16)
        by_high, by_mid, by_low = mm(c_all, b_high), mm(c_all[: 2 * NI], b_mid), mm(c_high, b_low)
        small = by_low + by_mid[NI:] + by_high[2 * NI :]
        wave_scr[:, j * CHUNK : (j + 1) * CHUNK] = small + (by_mid[:NI] + by_high[NI : 2 * NI]) + by_high[:NI]
    copies[1 + CHUNKS].wait()
    sine, cosine = sin_cos(wave_scr[...])
    opening = opening_ref[...]
    re = cosine * opening
    im = sine * opening
    for a in range(PU):
        pupil_ref[a * NI : (a + 1) * NI, 0:PU] = re[:, a * PU : (a + 1) * PU]
        pupil_ref[a * NI : (a + 1) * NI, 64 : 64 + PU] = im[:, a * PU : (a + 1) * PU]


def pack_kernel(object_hbm, data_hbm, coeffs_hbm, opening_hbm, basis_hbm, pr_hbm, pl_hbm, fl_hbm, fr_hbm,
                on_ref, off_ref, pupil_ref, pr_ref, pl_ref, fl_ref, fr_ref, on_scr, off_scr, send_sems, matrix_sems, *scratch):
    even = lax.axis_index("patch") % 2 == 0
    low, high = STRIDE - HALO, 0
    on_at = pl.multiple_of(jnp.where(even, low, high), 8)
    off_at = pl.multiple_of(jnp.where(even, high, low), 8)
    copies = fetch(
        [
            (object_hbm.at[pl.ds(off_at, HALO)], off_ref.at[pl.ds(0, HALO)]),
            (data_hbm.at[pl.ds(off_at, HALO)], off_scr),
            (object_hbm.at[pl.ds(on_at, HALO)], on_ref.at[pl.ds(0, HALO)]),
            (data_hbm.at[pl.ds(on_at, HALO)], on_scr),
        ],
        send_sems,
    )

    @pl.when(is_early())
    def _():
        matrices = fetch([(pr_hbm, pr_ref), (pl_hbm, pl_ref), (fl_hbm, fl_ref), (fr_hbm, fr_ref)], matrix_sems)
        pupil_part(coeffs_hbm, opening_hbm, basis_hbm, pupil_ref, *scratch)
        for copy in matrices:
            copy.wait()

    for copy in copies:
        copy.wait()
    for k in range(FK):
        rows = slice((k + 1) * HALO, (k + 2) * HALO)
        off_ref[rows, :] = off_scr[:, k, :]
        on_ref[rows, :] = on_scr[:, k, :]


def psf_kernel(pupil_in, pr_in, pl_in, fl_in, fr_in, coeffs_hbm, opening_hbm, basis_hbm, object_hbm, data_hbm, pr_hbm, pl_hbm, fl_hbm, fr_hbm,
               windows_hbm, rl_hbm, bl_hbm, br_hbm,
               pupil_ref, pr_ref, pl_ref, fl_ref, fr_ref, field_ref, spec_ref, scale_ref, ext, windows_ref, rl_ref, bl_ref, br_ref,
               rows_scr, left_scr, data_scr, sems, matrix_sems, *scratch):
    copies = fetch(
        [
            (object_hbm, ext.at[0, pl.ds(HALO, STRIDE), pl.ds(LANES, 2 * LANES)]),
            (data_hbm, data_scr), (windows_hbm, windows_ref), (rl_hbm, rl_ref), (bl_hbm, bl_ref), (br_hbm, br_ref),
        ],
        sems,
    )
    for i in range(1 + FK):
        ext[i, :, 0:LANES] = jnp.zeros((HEIGHT, LANES), F32)
        ext[i, :, 3 * LANES :] = jnp.zeros((HEIGHT, LANES), F32)
        ext[i, STRIDE + 2 * HALO :, LANES : 3 * LANES] = jnp.zeros((HEIGHT - STRIDE - 2 * HALO, 2 * LANES), F32)
    @pl.when(jnp.logical_not(is_early()))
    def _():
        matrices = fetch([(pr_hbm, pr_ref), (pl_hbm, pl_ref), (fl_hbm, fl_ref), (fr_hbm, fr_ref)], matrix_sems)
        pupil_part(coeffs_hbm, opening_hbm, basis_hbm, pupil_ref, *scratch)
        for copy in matrices:
            copy.wait()

    mixed = right(pupil_ref[...], pr_ref)
    rows_scr[0] = mixed[:, :LANES]
    rows_scr[1] = mixed[:, LANES:]
    for n in range(NI):
        lanes = slice(n * LANES, (n + 1) * LANES)
        left_scr[0:PU, lanes] = rows_scr[0, pl.ds(n, PU, stride=NI), :]
        left_scr[PU:, lanes] = rows_scr[1, pl.ds(n, PU, stride=NI), :]
    field = left(pl_ref, left_scr[...])
    field_ref[...] = field
    intensity = field[:PP] * field[:PP] + field[PP:] * field[PP:]
    sums = jnp.concatenate(
        [jnp.sum(intensity[:, n * LANES : (n + 1) * LANES], axis=0, keepdims=True) for n in range(NI)], axis=0
    )
    scale = 1.0 / jnp.sum(sums, axis=1, keepdims=True)
    scale_ref[...] = jnp.broadcast_to(scale, (NI, LANES))
    spread = jnp.concatenate(
        [intensity[:, n * LANES : (n + 1) * LANES] * scale[n : n + 1, :] for n in range(NI)], axis=1
    )
    pair = jnp.concatenate([spread[:, : PC * LANES], spread[:, PC * LANES :]], axis=0)
    spec_ref[...] = right(to_rows(left(fl_ref, pair)), fr_ref)
    for copy in copies:
        copy.wait()
    for k in range(FK):
        ext[k + 1, HALO : HALO + STRIDE, LANES : 3 * LANES] = data_scr[:, k, :]


def misfit_kernel(offsets_ref, kinds_ref, counts_ref, on_ref, off_ref, spec_ref, ext_in, windows_ref, rl_ref, fl_ref, fr_ref,
                  obj_spec_ref, res_spec_ref, centre_ref, on_rim_ref, off_rim_ref, ext, total):
    even = lax.axis_index("patch") % 2 == 0
    on_at = pl.multiple_of(jnp.where(even, STRIDE + HALO, 0), 8)
    off_at = pl.multiple_of(jnp.where(even, 0, STRIDE + HALO), 8)
    mid = slice(LANES, 3 * LANES)
    total[...] = jnp.zeros_like(total)
    for i in range(1 + FK):
        ext[i] = ext_in[i]
        ext[i, pl.ds(on_at, HALO), mid] = on_ref[i * HALO : (i + 1) * HALO, :]
        ext[i, pl.ds(off_at, HALO), mid] = off_ref[i * HALO : (i + 1) * HALO, :]

    row_base = [pl.multiple_of((offsets_ref[0, 0, c] >> 3) << 3, 8) for c in range(PC)]
    row_rest = [offsets_ref[0, 0, c] & 7 for c in range(PC)]
    base = [0, LANES, LANES, 2 * LANES]
    shift = [LANES + c * STRIDE - HALO - base[c] + offsets_ref[0, 1, c] for c in range(PC)]

    def cut(i, c):
        block = ext[i, pl.ds(row_base[c], TALL), base[c] : base[c] + 2 * LANES]
        moved = pltpu.roll(block, 2 * LANES - shift[c], 1)[:, :LANES]
        return pltpu.roll(moved, jnp.where(row_rest[c] == 0, 0, TALL - row_rest[c]), 0)[:PP]

    windows = [windows_ref[kinds_ref[0, c]] for c in range(PC)]
    weighted = jnp.concatenate([windows[c] * cut(0, c) for c in range(PC)], axis=1)
    obj = right(to_rows(left(rl_ref, weighted)), fr_ref)
    obj_spec_ref[...] = obj
    spec = spec_ref[...]
    o_re, o_im, s_re, s_im = obj[:, :LANES], obj[:, LANES:], spec[:, :LANES], spec[:, LANES:]
    taken = [jnp.concatenate([windows[c] * cut(k + 1, c) for c in range(PC)], axis=1) for k in range(FK)]
    data = right(to_rows(left(fl_ref, jnp.concatenate(taken, axis=0))), fr_ref)
    product = jnp.concatenate([o_re * s_re - o_im * s_im, o_re * s_im + o_im * s_re], axis=1)
    usable = [jnp.where(c < counts_ref[0, 0], 1.0, 0.0).astype(F32) for c in range(PC)]
    difference = product - data
    res = jnp.concatenate([difference[c * PP : (c + 1) * PP] * usable[c] for c in range(PC)], axis=0)
    res_spec_ref[...] = res
    r_re, r_im = res[:, :LANES], res[:, LANES:]
    back = jnp.concatenate([s_re * r_re + s_im * r_im, s_im * r_re - s_re * r_im], axis=1)
    grad = left(fl_ref[:PP, :], to_lanes(right(back, fr_ref)))
    for c in range(PC):
        mine = windows[c] * grad[:, c * LANES : (c + 1) * LANES] * (1.0 / (PP * PP))
        mine = pltpu.roll(jnp.concatenate([mine, jnp.zeros((TALL - PP, LANES), F32)], axis=0), row_rest[c], 0)
        placed = pltpu.roll(jnp.concatenate([mine, jnp.zeros((TALL, LANES), F32)], axis=1), shift[c], 1)
        rows, lanes = pl.ds(row_base[c], TALL), slice(base[c], base[c] + 2 * LANES)
        total[rows, lanes] = total[rows, lanes] + placed
    centre_ref[...] = total[HALO : HALO + STRIDE, mid]
    on_rim_ref[...] = total[pl.ds(on_at, HALO), mid]
    off_rim_ref[...] = total[pl.ds(off_at, HALO), mid]


def spread_grad_kernel(obj_spec_ref, res_spec_ref, fl_ref, fr_ref, grad_ref):
    obj, res = obj_spec_ref[...], res_spec_ref[...]
    o_re, o_im, r_re, r_im = obj[:, :LANES], obj[:, LANES:], res[:, :LANES], res[:, LANES:]
    back = jnp.concatenate([o_re * r_re + o_im * r_im, o_im * r_re - o_re * r_im], axis=1)
    grad_ref[...] = left(fl_ref, to_lanes(right(back, fr_ref)))


def phase_grad_kernel(grad_ref, field_ref, scale_ref, pupil_ref, bl_ref, br_ref, basis_hbm, flat_ref, basis_ref, rows_scr, sems):
    copies = fetch([(basis_hbm, basis_ref)], sems)
    re_parts, im_parts = [], []
    for n in range(NI):
        k, c = divmod(n, PC)
        lanes = slice(n * LANES, (n + 1) * LANES)
        f_re, f_im = field_ref[:PP, lanes], field_ref[PP:, lanes]
        scale = scale_ref[n : n + 1, :]
        spread = (f_re * f_re + f_im * f_im) * scale
        mine = grad_ref[k * PP : (k + 1) * PP, c * LANES : (c + 1) * LANES] * ((1 - 2 * k) / (PP * PP))
        mean = jnp.sum(jnp.sum(mine * spread, axis=0, keepdims=True), axis=1, keepdims=True)
        slope = 2.0 * scale * (mine - mean)
        re_parts.append(f_re * slope)
        im_parts.append(f_im * slope)
    wide = jnp.concatenate([jnp.concatenate(re_parts, axis=1), jnp.concatenate(im_parts, axis=1)], axis=0)
    half = left(bl_ref, wide)
    for n in range(NI):
        lanes = slice(n * LANES, (n + 1) * LANES)
        rows_scr[0, pl.ds(n, PU, stride=NI), :] = half[:PU, lanes]
        rows_scr[1, pl.ds(n, PU, stride=NI), :] = half[PU:, lanes]
    pupil_grad = right(jnp.concatenate([rows_scr[0], rows_scr[1]], axis=1), br_ref)
    pupil = pupil_ref[...]
    crossed = pupil * pltpu.roll(pupil_grad, 64, 1)
    slopes = crossed - pltpu.roll(crossed, 64, 1)
    for a in range(PU):
        flat_ref[:, a * PU : (a + 1) * PU] = slopes[a * NI : (a + 1) * NI, 0:PU]
    copies[0].wait()


def mode_kernel(flat_ref, basis_ref, out_ref):
    high, low = split(flat_ref[...])
    b_high, b_low = split(basis_ref[...])

    def by_modes(a, b):
        return lax.dot_general(a, b, (((1,), (1,)), ((), ())), preferred_element_type=F32)

    first = by_modes(jnp.concatenate([high, low], axis=0), b_high)
    out = first[:NI] + first[NI:] + by_modes(high, b_low)
    out_ref[0, 0] = out[:PC]
    out_ref[1, 0] = out[PC:]


def call(kernel, out_shapes, scratch=(), smem=0, near=0, far=0, aliases=None, name=None):
    vmem = pl.BlockSpec(memory_space=pltpu.VMEM)
    inner = pl.pallas_call(
        kernel,
        out_shape=out_shapes,
        in_specs=[pl.BlockSpec(memory_space=pltpu.SMEM)] * smem + [vmem] * near + [pl.BlockSpec(memory_space=pltpu.HBM)] * far,
        out_specs=jax.tree.map(lambda _: vmem, out_shapes),
        scratch_shapes=list(scratch),
        input_output_aliases=aliases or {},
        compiler_params=pltpu.CompilerParams(vmem_limit_bytes=VMEM_LIMIT),
        name=name,
    )

    def run(*operands):
        placed = list(operands)
        for i in range(smem + near, smem + near + far):
            placed[i] = pltpu.with_memory_space_constraint(placed[i], pltpu.HBM)
        for i in range(smem, smem + near):
            placed[i] = pltpu.with_memory_space_constraint(placed[i], pltpu.VMEM)
        return inner(*placed)

    return run


def shape(*dims):
    return pltpu.VMEM(dims, F32)


def sems(count):
    return pltpu.SemaphoreType.DMA((count,))


def like(value):
    return pltpu.VMEM(value.shape, BF16 if value.dtype == ml_dtypes.bfloat16 else F32)


def swap_on(values):
    count = lax.axis_size("patch")
    return lax.ppermute(values, "patch", [(i, i ^ 1) for i in range(count)])


def swap_off(values):
    count = lax.axis_size("patch")
    pairs = [(i, i + 1) for i in range(1, count - 1, 2)]
    return lax.ppermute(values, "patch", pairs + [(j, i) for i, j in pairs])


def swap_frames(values, bit):
    count = lax.axis_size("frames")
    return lax.ppermute(values, "frames", [(i, i ^ bit) for i in range(count)])


def body(object_band, data_band, coeffs, mode_basis, offsets, window_ids, counts):
    columns = object_band.shape[1]
    host = constants()
    const = {name: jnp.asarray(value) for name, value in host.items()}
    room = {name: like(value) for name, value in host.items()}
    halo_room = pltpu.VMEM((HALO, FK, columns), F32)
    pupil_room = [
        pltpu.VMEM((CHUNKS, MODES, CHUNK), F32), pltpu.VMEM((NI, PU * PU), F32), pltpu.VMEM((FK, 1, PC, MODES), F32),
        room["opening"], sems(CHUNKS + 2),
    ]
    wave_given = (coeffs, const["opening"], mode_basis)
    early_matrices = ("pupil_right", "pupil_left", "fwd_left", "fwd_right")
    matrices = [const[name] for name in early_matrices]
    made_early = [shape(PU * NI, LANES)] + [room[name] for name in early_matrices]
    on_send, off_send, *early = call(
        pack_kernel, [shape(3 * HALO, columns)] * 2 + made_early,
        scratch=[halo_room, halo_room, sems(4), sems(4)] + pupil_room, far=9, name="pack",
    )(object_band, data_band, *wave_given, *matrices)
    on_halo = swap_on(on_send)
    off_halo = swap_off(off_send)
    kept = ("windows", "real_left", "back_left", "back_right")
    pupil, _, _, fwd_left, fwd_right, field, spec, scale, ext, *kept_values = call(
        psf_kernel,
        made_early + [shape(2 * PP, NI * LANES), shape(PC * PP, 2 * LANES), shape(NI, LANES), shape(1 + FK, HEIGHT, 4 * LANES)]
        + [room[name] for name in kept],
        scratch=[
            pltpu.VMEM((2, PU * NI, LANES), F32), pltpu.VMEM((2 * PU, NI * LANES), F32), pltpu.VMEM((STRIDE, FK, columns), F32),
            sems(6), sems(4),
        ] + pupil_room,
        near=5,
        far=13,
        aliases={i: i for i in range(5)},
        name="psf",
    )(*early, *wave_given, object_band, data_band, *matrices, *[const[name] for name in kept])
    here = dict(zip(kept, kept_values))
    obj_spec, res_spec, centre, on_rim, off_rim = call(
        misfit_kernel,
        [shape(PC * PP, 2 * LANES)] * 2 + [shape(STRIDE, columns), shape(HALO, columns), shape(HALO, columns)],
        scratch=[pltpu.VMEM((1 + FK, HEIGHT, 4 * LANES), F32), pltpu.VMEM((HEIGHT, 4 * LANES), F32)],
        smem=3,
        near=8,
        name="misfit",
    )(
        jnp.transpose(offsets, (0, 2, 1)), window_ids, counts.reshape(1, 1), on_halo, off_halo, spec, ext,
        here["windows"], here["real_left"], fwd_left, fwd_right,
    )
    on_rim = swap_on(on_rim)
    off_rim = swap_off(off_rim)
    spread_grad = call(spread_grad_kernel, shape(2 * PP, PC * LANES), near=4, name="spread_grad")(
        obj_spec, res_spec, fwd_left, fwd_right
    )
    even = lax.axis_index("patch") % 2 == 0
    upper = jnp.where(even, off_rim, on_rim)
    lower = jnp.where(even, on_rim, off_rim)
    rows = jnp.concatenate([centre[:HALO] + upper, centre[HALO : STRIDE - HALO], centre[STRIDE - HALO :] + lower], axis=0)
    rows, spread_grad = lax.optimization_barrier((rows, spread_grad))
    moved = swap_frames(rows, 4)
    flat, basis = call(
        phase_grad_kernel, [shape(NI, PU * PU), shape(*mode_basis.shape)],
        scratch=[pltpu.VMEM((2, PU * NI, LANES), F32), sems(1)], near=6, far=1, name="phase_grad",
    )(spread_grad, field, scale, pupil, here["back_left"], here["back_right"], mode_basis)
    rows = rows + moved
    rows, flat = lax.optimization_barrier((rows, flat))
    coeff_grad = call(mode_kernel, jax.ShapeDtypeStruct((FK, 1, PC, MODES), F32), near=2, name="modes")(flat, basis)
    rows = rows + swap_frames(rows, 1) + swap_frames(rows, 2) + swap_frames(rows, 3)
    return rows, coeff_grad


def solution(mesh):
    in_specs = (
        P("patch", None),
        P("patch", "frames", None),
        P("frames", "patch", None, None),
        P(),
        P("patch", None, None),
        P("patch", None),
        P("patch"),
    )
    out_specs = (P("patch", None), P("frames", "patch", None, None))
    return jax.shard_map(body, mesh=mesh, in_specs=in_specs, out_specs=out_specs, check_vma=False)
```

```python
import math

import jax
import jax.numpy as jnp
import ml_dtypes
import numpy as np
from jax import lax
from jax.experimental import pallas as pl
from jax.experimental.pallas import tpu as pltpu
from jax.sharding import PartitionSpec as P

PP = 96
PU = 48
STRIDE = 64
HALO = 24
PC = 4
FK = 2
NI = PC * FK
LANES = 128
MODES = 200
TALL = PP + 8
HEIGHT = STRIDE + 2 * HALO + 8
F32 = jnp.float32
BF16 = jnp.bfloat16
VMEM_LIMIT = 16 * 1024 * 1024
CHUNK = 768
CHUNKS = PU * PU // CHUNK


def halves(matrix):
    high = matrix.astype(ml_dtypes.bfloat16)
    low = (matrix - high.astype(np.float64)).astype(ml_dtypes.bfloat16)
    return high, low


def dft(points, length):
    turns = np.outer(np.arange(points), np.arange(length)) % points
    angles = 2.0 * math.pi / points * turns
    return np.cos(angles), -np.sin(angles)


def constants():
    full_re, full_im = dft(PP, PP)
    half_re, half_im = dft(PP, PU)
    fwd_right = np.zeros((256, 256))
    fwd_right[:96, :96] = full_re
    fwd_right[128:224, :96] = -full_im
    fwd_right[:96, 128:224] = full_im
    fwd_right[128:224, 128:224] = full_re
    pupil_right = np.zeros((128, 256))
    pupil_right[:48, :96] = half_re.T
    pupil_right[64:112, :96] = -half_im.T
    pupil_right[:48, 128:224] = half_im.T
    pupil_right[64:112, 128:224] = half_re.T
    pupil_left = np.block([[half_re, -half_im], [half_im, half_re]])
    fwd_left = np.block([[full_re, -full_im], [full_im, full_re]])
    real_left = np.concatenate([full_re, full_im], axis=0)

    def tall(matrix):
        high, low = halves(matrix)
        return np.concatenate([high, low, high], axis=0)

    def wide(matrix):
        high, low = halves(matrix)
        return np.concatenate([high, low, high], axis=1)

    side = np.arange(PP) + 0.5
    windows = np.zeros((4, PP, LANES), np.float32)
    for kind in range(4):
        edge = float(max(PP * (kind + 1) // 12, 1))
        rising = 0.5 - 0.5 * np.cos(math.pi * np.minimum(side, edge) / edge)
        profile = rising * rising[::-1]
        windows[kind, :, :PP] = np.outer(profile, profile)
    centre = np.arange(PU) + 0.5 - 0.5 * PU
    opening = (centre[:, None] ** 2 + centre[None, :] ** 2 <= (0.5 * PU) ** 2).reshape(1, PU * PU)
    return {
        "fwd_right": tall(fwd_right),
        "pupil_right": tall(pupil_right),
        "pupil_left": wide(pupil_left),
        "fwd_left": wide(fwd_left),
        "real_left": wide(real_left),
        "back_left": wide(pupil_left.T),
        "back_right": tall(pupil_right.T),
        "windows": windows,
        "opening": opening.astype(np.float32),
    }


def split(values):
    high = values.astype(BF16)
    return high, (values - high.astype(F32)).astype(BF16)


def mm(a, b):
    return jnp.dot(a, b, preferred_element_type=F32)


def right(values, matrix):
    high, low = split(values)
    return mm(jnp.concatenate([high, high, low], axis=1), matrix[...])


def left(matrix, values):
    high, low = split(values)
    return mm(matrix[...], jnp.concatenate([high, high, low], axis=0))


def to_rows(spectrum):
    parts = []
    for c in range(spectrum.shape[1] // LANES):
        lanes = slice(c * LANES, (c + 1) * LANES)
        parts.append(jnp.concatenate([spectrum[:PP, lanes], spectrum[PP:, lanes]], axis=1))
    return jnp.concatenate(parts, axis=0)


def to_lanes(rows):
    count = rows.shape[0] // PP
    re = jnp.concatenate([rows[c * PP : (c + 1) * PP, :LANES] for c in range(count)], axis=1)
    im = jnp.concatenate([rows[c * PP : (c + 1) * PP, LANES:] for c in range(count)], axis=1)
    return jnp.concatenate([re, im], axis=0)


def sin_cos(angle):
    turns = jnp.floor(angle * (2.0 / math.pi) + 0.5)
    rest = angle - turns * 1.5703125
    rest = rest - turns * 4.837512969970703125e-4
    rest = rest - turns * 7.54978995489188216e-8
    sq = rest * rest
    sine = ((-1.9515295891e-4 * sq + 8.3321608736e-3) * sq - 1.6666654611e-1) * sq * rest + rest
    cosine = ((2.443315711809948e-5 * sq - 1.388731625493765e-3) * sq + 4.166664568298827e-2) * sq * sq - 0.5 * sq + 1.0
    quarter = turns.astype(jnp.int32) & 3
    swapped = (quarter & 1) == 1
    sin_now = jnp.where(swapped, cosine, sine)
    cos_now = jnp.where(swapped, sine, cosine)
    sin_now = jnp.where(quarter >= 2, -sin_now, sin_now)
    cos_now = jnp.where((quarter == 1) | (quarter == 2), -cos_now, cos_now)
    return sin_now, cos_now


def fetch(pairs, sems):
    copies = [pltpu.make_async_copy(src, dst, sems.at[i]) for i, (src, dst) in enumerate(pairs)]
    for copy in copies:
        copy.start()
    return copies


def is_early():
    return lax.axis_index("patch") % 8 == 0


def pupil_part(coeffs_hbm, opening_hbm, basis_hbm, pupil_ref, basis_scr, wave_scr, coeffs_ref, opening_ref, sems, later):
    copies = fetch(
        [(coeffs_hbm, coeffs_ref)]
        + [(basis_hbm.at[:, pl.ds(j * CHUNK, CHUNK)], basis_scr.at[j]) for j in range(CHUNKS)]
        + [(opening_hbm, opening_ref)],
        sems,
    )
    late_copies = fetch(*later)
    pupil_ref[...] = jnp.zeros_like(pupil_ref)
    copies[0].wait()
    coeffs = jnp.concatenate([coeffs_ref[0, 0], coeffs_ref[1, 0]], axis=0)
    c_high = coeffs.astype(BF16)
    rest = coeffs - c_high.astype(F32)
    c_mid = rest.astype(BF16)
    c_low = (rest - c_mid.astype(F32)).astype(BF16)
    c_all = jnp.concatenate([c_high, c_mid, c_low], axis=0)
    for j in range(CHUNKS):
        copies[1 + j].wait()
        basis = basis_scr[j]
        b_high = basis.astype(BF16)
        b_rest = basis - b_high.astype(F32)
        b_mid = b_rest.astype(BF16)
        b_low = (b_rest - b_mid.astype(F32)).astype(BF16)
        by_high, by_mid, by_low = mm(c_all, b_high), mm(c_all[: 2 * NI], b_mid), mm(c_high, b_low)
        small = by_low + by_mid[NI:] + by_high[2 * NI :]
        wave_scr[:, j * CHUNK : (j + 1) * CHUNK] = small + (by_mid[:NI] + by_high[NI : 2 * NI]) + by_high[:NI]
    copies[1 + CHUNKS].wait()
    sine, cosine = sin_cos(wave_scr[...])
    opening = opening_ref[...]
    re = cosine * opening
    im = sine * opening
    for a in range(PU):
        pupil_ref[a * NI : (a + 1) * NI, 0:PU] = re[:, a * PU : (a + 1) * PU]
        pupil_ref[a * NI : (a + 1) * NI, 64 : 64 + PU] = im[:, a * PU : (a + 1) * PU]
    for copy in late_copies:
        copy.wait()


def pack_kernel(object_hbm, data_hbm, coeffs_hbm, opening_hbm, basis_hbm, pr_hbm, pl_hbm, fl_hbm, fr_hbm,
                on_ref, off_ref, pupil_ref, pr_ref, pl_ref, fl_ref, fr_ref, on_scr, off_scr, send_sems, matrix_sems, *scratch):
    even = lax.axis_index("patch") % 2 == 0
    low, high = STRIDE - HALO, 0
    on_at = pl.multiple_of(jnp.where(even, low, high), 8)
    off_at = pl.multiple_of(jnp.where(even, high, low), 8)
    copies = fetch(
        [
            (object_hbm.at[pl.ds(off_at, HALO)], off_ref.at[pl.ds(0, HALO)]),
            (data_hbm.at[pl.ds(off_at, HALO)], off_scr),
            (object_hbm.at[pl.ds(on_at, HALO)], on_ref.at[pl.ds(0, HALO)]),
            (data_hbm.at[pl.ds(on_at, HALO)], on_scr),
        ],
        send_sems,
    )

    @pl.when(is_early())
    def _():
        matrices = [(pr_hbm, pr_ref), (pl_hbm, pl_ref), (fl_hbm, fl_ref), (fr_hbm, fr_ref)]
        pupil_part(coeffs_hbm, opening_hbm, basis_hbm, pupil_ref, *scratch, (matrices, matrix_sems))

    for copy in copies:
        copy.wait()
    for k in range(FK):
        rows = slice((k + 1) * HALO, (k + 2) * HALO)
        off_ref[rows, :] = off_scr[:, k, :]
        on_ref[rows, :] = on_scr[:, k, :]


def psf_kernel(pupil_in, pr_in, pl_in, fl_in, fr_in, coeffs_hbm, opening_hbm, basis_hbm, object_hbm, data_hbm, pr_hbm, pl_hbm, fl_hbm, fr_hbm,
               windows_hbm, rl_hbm, bl_hbm, br_hbm,
               pupil_ref, pr_ref, pl_ref, fl_ref, fr_ref, field_ref, spec_ref, scale_ref, ext, windows_ref, rl_ref, bl_ref, br_ref,
               rows_scr, left_scr, data_scr, sems, matrix_sems, *scratch):
    copies = fetch(
        [
            (object_hbm, ext.at[0, pl.ds(HALO, STRIDE), pl.ds(LANES, 2 * LANES)]),
            (data_hbm, data_scr), (windows_hbm, windows_ref), (rl_hbm, rl_ref), (bl_hbm, bl_ref), (br_hbm, br_ref),
        ],
        sems,
    )
    for i in range(1 + FK):
        ext[i, :, 0:LANES] = jnp.zeros((HEIGHT, LANES), F32)
        ext[i, :, 3 * LANES :] = jnp.zeros((HEIGHT, LANES), F32)
        ext[i, STRIDE + 2 * HALO :, LANES : 3 * LANES] = jnp.zeros((HEIGHT - STRIDE - 2 * HALO, 2 * LANES), F32)
    @pl.when(jnp.logical_not(is_early()))
    def _():
        matrices = [(pr_hbm, pr_ref), (pl_hbm, pl_ref), (fl_hbm, fl_ref), (fr_hbm, fr_ref)]
        pupil_part(coeffs_hbm, opening_hbm, basis_hbm, pupil_ref, *scratch, (matrices, matrix_sems))

    mixed = right(pupil_ref[...], pr_ref)
    rows_scr[0] = mixed[:, :LANES]
    rows_scr[1] = mixed[:, LANES:]
    for n in range(NI):
        lanes = slice(n * LANES, (n + 1) * LANES)
        left_scr[0:PU, lanes] = rows_scr[0, pl.ds(n, PU, stride=NI), :]
        left_scr[PU:, lanes] = rows_scr[1, pl.ds(n, PU, stride=NI), :]
    field = left(pl_ref, left_scr[...])
    field_ref[...] = field
    intensity = field[:PP] * field[:PP] + field[PP:] * field[PP:]
    sums = jnp.concatenate(
        [jnp.sum(intensity[:, n * LANES : (n + 1) * LANES], axis=0, keepdims=True) for n in range(NI)], axis=0
    )
    scale = 1.0 / jnp.sum(sums, axis=1, keepdims=True)
    scale_ref[...] = jnp.broadcast_to(scale, (NI, LANES))
    spread = jnp.concatenate(
        [intensity[:, n * LANES : (n + 1) * LANES] * scale[n : n + 1, :] for n in range(NI)], axis=1
    )
    pair = jnp.concatenate([spread[:, : PC * LANES], spread[:, PC * LANES :]], axis=0)
    spec_ref[...] = right(to_rows(left(fl_ref, pair)), fr_ref)
    for copy in copies:
        copy.wait()
    for k in range(FK):
        ext[k + 1, HALO : HALO + STRIDE, LANES : 3 * LANES] = data_scr[:, k, :]


def misfit_kernel(offsets_ref, kinds_ref, counts_ref, off_ref, on_ref, spec_ref, ext_in, windows_ref, rl_ref, fl_ref, fr_ref,
                  obj_spec_ref, res_spec_ref, centre_ref, on_rim_ref, off_rim_ref, ext, total):
    even = lax.axis_index("patch") % 2 == 0
    on_at = pl.multiple_of(jnp.where(even, STRIDE + HALO, 0), 8)
    off_at = pl.multiple_of(jnp.where(even, 0, STRIDE + HALO), 8)
    mid = slice(LANES, 3 * LANES)
    total[...] = jnp.zeros_like(total)
    for i in range(1 + FK):
        ext[i] = ext_in[i]
        ext[i, pl.ds(on_at, HALO), mid] = on_ref[i * HALO : (i + 1) * HALO, :]
        ext[i, pl.ds(off_at, HALO), mid] = off_ref[i * HALO : (i + 1) * HALO, :]

    row_base = [pl.multiple_of((offsets_ref[0, 0, c] >> 3) << 3, 8) for c in range(PC)]
    row_rest = [offsets_ref[0, 0, c] & 7 for c in range(PC)]
    base = [0, LANES, LANES, 2 * LANES]
    shift = [LANES + c * STRIDE - HALO - base[c] + offsets_ref[0, 1, c] for c in range(PC)]

    def cut(i, c):
        block = ext[i, pl.ds(row_base[c], TALL), base[c] : base[c] + 2 * LANES]
        moved = pltpu.roll(block, 2 * LANES - shift[c], 1)[:, :LANES]
        return pltpu.roll(moved, jnp.where(row_rest[c] == 0, 0, TALL - row_rest[c]), 0)[:PP]

    pairs = [(0, 1), (2, 3)]
    windows = [windows_ref[kinds_ref[0, c]] for c in range(PC)]
    weighted = [jnp.concatenate([windows[c] * cut(0, c) for c in pair], axis=1) for pair in pairs]
    taken = [
        jnp.concatenate([jnp.concatenate([windows[c] * cut(k + 1, c) for c in pair], axis=1) for k in range(FK)], axis=0)
        for pair in pairs
    ]
    obj_left = [left(rl_ref, values) for values in weighted]
    data_left = [left(fl_ref, values) for values in taken]
    obj = [right(to_rows(values), fr_ref) for values in obj_left]
    data = [right(to_rows(values), fr_ref) for values in data_left]
    back = []
    for g, pair in enumerate(pairs):
        rows = slice(pair[0] * PP, (pair[-1] + 1) * PP)
        obj_spec_ref[rows, :] = obj[g]
        o_re, o_im, s_re, s_im = obj[g][:, :LANES], obj[g][:, LANES:], spec_ref[rows, :LANES], spec_ref[rows, LANES:]
        product = jnp.concatenate([o_re * s_re - o_im * s_im, o_re * s_im + o_im * s_re], axis=1)
        usable = [jnp.where(c < counts_ref[0, 0], 1.0, 0.0).astype(F32) for c in pair]
        difference = product - data[g]
        res = jnp.concatenate([difference[i * PP : (i + 1) * PP] * usable[i] for i in range(len(pair))], axis=0)
        res_spec_ref[rows, :] = res
        r_re, r_im = res[:, :LANES], res[:, LANES:]
        back.append(jnp.concatenate([s_re * r_re + s_im * r_im, s_im * r_re - s_re * r_im], axis=1))
    mixed = [to_lanes(right(values, fr_ref)) for values in back]
    grad = jnp.concatenate([left(fl_ref[:PP, :], values) for values in mixed], axis=1)
    for c in range(PC):
        mine = windows[c] * grad[:, c * LANES : (c + 1) * LANES] * (1.0 / (PP * PP))
        mine = pltpu.roll(jnp.concatenate([mine, jnp.zeros((TALL - PP, LANES), F32)], axis=0), row_rest[c], 0)
        placed = pltpu.roll(jnp.concatenate([mine, jnp.zeros((TALL, LANES), F32)], axis=1), shift[c], 1)
        rows, lanes = pl.ds(row_base[c], TALL), slice(base[c], base[c] + 2 * LANES)
        total[rows, lanes] = total[rows, lanes] + placed
    centre_ref[...] = total[HALO : HALO + STRIDE, mid]
    on_rim_ref[...] = total[pl.ds(on_at, HALO), mid]
    off_rim_ref[...] = total[pl.ds(off_at, HALO), mid]


def spread_grad_kernel(obj_spec_ref, res_spec_ref, fl_ref, fr_ref, grad_ref):
    obj, res = obj_spec_ref[...], res_spec_ref[...]
    o_re, o_im, r_re, r_im = obj[:, :LANES], obj[:, LANES:], res[:, :LANES], res[:, LANES:]
    back = jnp.concatenate([o_re * r_re + o_im * r_im, o_im * r_re - o_re * r_im], axis=1)
    grad_ref[...] = left(fl_ref, to_lanes(right(back, fr_ref)))


def phase_grad_kernel(grad_ref, field_ref, scale_ref, pupil_ref, bl_ref, br_ref, basis_hbm, flat_ref, basis_ref, rows_scr, sems):
    copies = fetch([(basis_hbm, basis_ref)], sems)
    re_parts, im_parts = [], []
    for n in range(NI):
        k, c = divmod(n, PC)
        lanes = slice(n * LANES, (n + 1) * LANES)
        f_re, f_im = field_ref[:PP, lanes], field_ref[PP:, lanes]
        scale = scale_ref[n : n + 1, :]
        spread = (f_re * f_re + f_im * f_im) * scale
        mine = grad_ref[k * PP : (k + 1) * PP, c * LANES : (c + 1) * LANES] * ((1 - 2 * k) / (PP * PP))
        mean = jnp.sum(jnp.sum(mine * spread, axis=0, keepdims=True), axis=1, keepdims=True)
        slope = 2.0 * scale * (mine - mean)
        re_parts.append(f_re * slope)
        im_parts.append(f_im * slope)
    wide = jnp.concatenate([jnp.concatenate(re_parts, axis=1), jnp.concatenate(im_parts, axis=1)], axis=0)
    half = left(bl_ref, wide)
    for n in range(NI):
        lanes = slice(n * LANES, (n + 1) * LANES)
        rows_scr[0, pl.ds(n, PU, stride=NI), :] = half[:PU, lanes]
        rows_scr[1, pl.ds(n, PU, stride=NI), :] = half[PU:, lanes]
    pupil_grad = right(jnp.concatenate([rows_scr[0], rows_scr[1]], axis=1), br_ref)
    pupil = pupil_ref[...]
    crossed = pupil * pltpu.roll(pupil_grad, 64, 1)
    slopes = crossed - pltpu.roll(crossed, 64, 1)
    for a in range(PU):
        flat_ref[:, a * PU : (a + 1) * PU] = slopes[a * NI : (a + 1) * NI, 0:PU]
    copies[0].wait()


def mode_kernel(flat_ref, basis_ref, out_ref):
    high, low = split(flat_ref[...])
    b_high, b_low = split(basis_ref[...])

    def by_modes(a, b):
        return lax.dot_general(a, b, (((1,), (1,)), ((), ())), preferred_element_type=F32)

    first = by_modes(jnp.concatenate([high, low], axis=0), b_high)
    out = first[:NI] + first[NI:] + by_modes(high, b_low)
    out_ref[0, 0] = out[:PC]
    out_ref[1, 0] = out[PC:]


def call(kernel, out_shapes, scratch=(), smem=0, near=0, far=0, aliases=None, name=None):
    vmem = pl.BlockSpec(memory_space=pltpu.VMEM)
    inner = pl.pallas_call(
        kernel,
        out_shape=out_shapes,
        in_specs=[pl.BlockSpec(memory_space=pltpu.SMEM)] * smem + [vmem] * near + [pl.BlockSpec(memory_space=pltpu.HBM)] * far,
        out_specs=jax.tree.map(lambda _: vmem, out_shapes),
        scratch_shapes=list(scratch),
        input_output_aliases=aliases or {},
        compiler_params=pltpu.CompilerParams(vmem_limit_bytes=VMEM_LIMIT),
        name=name,
    )

    def run(*operands):
        placed = list(operands)
        for i in range(smem + near, smem + near + far):
            placed[i] = pltpu.with_memory_space_constraint(placed[i], pltpu.HBM)
        for i in range(smem, smem + near):
            placed[i] = pltpu.with_memory_space_constraint(placed[i], pltpu.VMEM)
        return inner(*placed)

    return run


def shape(*dims):
    return pltpu.VMEM(dims, F32)


def sems(count):
    return pltpu.SemaphoreType.DMA((count,))


def like(value):
    return pltpu.VMEM(value.shape, BF16 if value.dtype == ml_dtypes.bfloat16 else F32)


def swap_on(values):
    count = lax.axis_size("patch")
    return lax.ppermute(values, "patch", [(i, i ^ 1) for i in range(count)])


def swap_off(values):
    count = lax.axis_size("patch")
    pairs = [(i, i + 1) for i in range(1, count - 1, 2)]
    return lax.ppermute(values, "patch", pairs + [(j, i) for i, j in pairs])


def swap_frames(values, bit):
    count = lax.axis_size("frames")
    return lax.ppermute(values, "frames", [(i, i ^ bit) for i in range(count)])


def body(object_band, data_band, coeffs, mode_basis, offsets, window_ids, counts):
    columns = object_band.shape[1]
    host = constants()
    const = {name: jnp.asarray(value) for name, value in host.items()}
    room = {name: like(value) for name, value in host.items()}
    halo_room = pltpu.VMEM((HALO, FK, columns), F32)
    pupil_room = [
        pltpu.VMEM((CHUNKS, MODES, CHUNK), F32), pltpu.VMEM((NI, PU * PU), F32), pltpu.VMEM((FK, 1, PC, MODES), F32),
        room["opening"], sems(CHUNKS + 2),
    ]
    wave_given = (coeffs, const["opening"], mode_basis)
    early_matrices = ("pupil_right", "pupil_left", "fwd_left", "fwd_right")
    matrices = [const[name] for name in early_matrices]
    made_early = [shape(PU * NI, LANES)] + [room[name] for name in early_matrices]
    on_send, off_send, *early = call(
        pack_kernel, [shape(3 * HALO, columns)] * 2 + made_early,
        scratch=[halo_room, halo_room, sems(4), sems(4)] + pupil_room, far=9, name="pack",
    )(object_band, data_band, *wave_given, *matrices)
    on_halo = swap_on(on_send)
    off_halo = swap_off(off_send)
    kept = ("windows", "real_left", "back_left", "back_right")
    pupil, _, _, fwd_left, fwd_right, field, spec, scale, ext, *kept_values = call(
        psf_kernel,
        made_early + [shape(2 * PP, NI * LANES), shape(PC * PP, 2 * LANES), shape(NI, LANES), shape(1 + FK, HEIGHT, 4 * LANES)]
        + [room[name] for name in kept],
        scratch=[
            pltpu.VMEM((2, PU * NI, LANES), F32), pltpu.VMEM((2 * PU, NI * LANES), F32), pltpu.VMEM((STRIDE, FK, columns), F32),
            sems(6), sems(4),
        ] + pupil_room,
        near=5,
        far=13,
        aliases={i: i for i in range(5)},
        name="psf",
    )(*early, *wave_given, object_band, data_band, *matrices, *[const[name] for name in kept])
    here = dict(zip(kept, kept_values))
    obj_spec, res_spec, centre, on_rim, off_rim = call(
        misfit_kernel,
        [shape(PC * PP, 2 * LANES)] * 2 + [shape(STRIDE, columns), shape(HALO, columns), shape(HALO, columns)],
        scratch=[pltpu.VMEM((1 + FK, HEIGHT, 4 * LANES), F32), pltpu.VMEM((HEIGHT, 4 * LANES), F32)],
        smem=3,
        near=8,
        name="misfit",
    )(
        jnp.transpose(offsets, (0, 2, 1)), window_ids, counts.reshape(1, 1), off_halo, on_halo, spec, ext,
        here["windows"], here["real_left"], fwd_left, fwd_right,
    )
    on_rim = swap_on(on_rim)
    off_rim = swap_off(off_rim)
    spread_grad = call(spread_grad_kernel, shape(2 * PP, PC * LANES), near=4, name="spread_grad")(
        obj_spec, res_spec, fwd_left, fwd_right
    )
    even = lax.axis_index("patch") % 2 == 0
    upper = jnp.where(even, off_rim, on_rim)
    lower = jnp.where(even, on_rim, off_rim)
    rows = jnp.concatenate([centre[:HALO] + upper, centre[HALO : STRIDE - HALO], centre[STRIDE - HALO :] + lower], axis=0)
    rows, spread_grad = lax.optimization_barrier((rows, spread_grad))
    moved = swap_frames(rows, 5) + swap_frames(rows, 4) + swap_frames(rows, 1)
    flat, basis = call(
        phase_grad_kernel, [shape(NI, PU * PU), shape(*mode_basis.shape)],
        scratch=[pltpu.VMEM((2, PU * NI, LANES), F32), sems(1)], near=6, far=1, name="phase_grad",
    )(spread_grad, field, scale, pupil, here["back_left"], here["back_right"], mode_basis)
    rows = rows + moved
    rows, flat = lax.optimization_barrier((rows, flat))
    coeff_grad = call(mode_kernel, jax.ShapeDtypeStruct((FK, 1, PC, MODES), F32), near=2, name="modes")(flat, basis)
    rows = rows + swap_frames(rows, 3)
    return rows, coeff_grad


def solution(mesh):
    in_specs = (
        P("patch", None),
        P("patch", "frames", None),
        P("frames", "patch", None, None),
        P(),
        P("patch", None, None),
        P("patch", None),
        P("patch"),
    )
    out_specs = (P("patch", None), P("frames", "patch", None, None))
    return jax.shard_map(body, mesh=mesh, in_specs=in_specs, out_specs=out_specs, check_vma=False)
```

```python
import math

import jax
import jax.numpy as jnp
import ml_dtypes
import numpy as np
from jax import lax
from jax.experimental import pallas as pl
from jax.experimental.pallas import tpu as pltpu
from jax.sharding import PartitionSpec as P

PP = 96
PU = 48
STRIDE = 64
HALO = 24
PC = 4
FK = 2
NI = PC * FK
LANES = 128
MODES = 200
TALL = PP + 8
HEIGHT = STRIDE + 2 * HALO + 8
F32 = jnp.float32
BF16 = jnp.bfloat16
VMEM_LIMIT = 16 * 1024 * 1024
CHUNK = 768
CHUNKS = PU * PU // CHUNK


def halves(matrix):
    high = matrix.astype(ml_dtypes.bfloat16)
    low = (matrix - high.astype(np.float64)).astype(ml_dtypes.bfloat16)
    return high, low


def dft(points, length):
    turns = np.outer(np.arange(points), np.arange(length)) % points
    angles = 2.0 * math.pi / points * turns
    return np.cos(angles), -np.sin(angles)


def constants():
    full_re, full_im = dft(PP, PP)
    half_re, half_im = dft(PP, PU)
    fwd_right = np.zeros((256, 256))
    fwd_right[:96, :96] = full_re
    fwd_right[128:224, :96] = -full_im
    fwd_right[:96, 128:224] = full_im
    fwd_right[128:224, 128:224] = full_re
    pupil_right = np.zeros((128, 256))
    pupil_right[:48, :96] = half_re.T
    pupil_right[64:112, :96] = -half_im.T
    pupil_right[:48, 128:224] = half_im.T
    pupil_right[64:112, 128:224] = half_re.T
    pupil_left = np.block([[half_re, -half_im], [half_im, half_re]])
    fwd_left = np.block([[full_re, -full_im], [full_im, full_re]])
    real_left = np.concatenate([full_re, full_im], axis=0)

    def tall(matrix):
        high, low = halves(matrix)
        return np.concatenate([high, low, high], axis=0)

    def wide(matrix):
        high, low = halves(matrix)
        return np.concatenate([high, low, high], axis=1)

    side = np.arange(PP) + 0.5
    windows = np.zeros((4, PP, LANES), np.float32)
    for kind in range(4):
        edge = float(max(PP * (kind + 1) // 12, 1))
        rising = 0.5 - 0.5 * np.cos(math.pi * np.minimum(side, edge) / edge)
        profile = rising * rising[::-1]
        windows[kind, :, :PP] = np.outer(profile, profile)
    centre = np.arange(PU) + 0.5 - 0.5 * PU
    opening = (centre[:, None] ** 2 + centre[None, :] ** 2 <= (0.5 * PU) ** 2).reshape(1, PU * PU)
    return {
        "fwd_right": tall(fwd_right),
        "pupil_right": tall(pupil_right),
        "pupil_left": wide(pupil_left),
        "fwd_left": wide(fwd_left),
        "real_left": wide(real_left),
        "back_left": wide(pupil_left.T),
        "back_right": tall(pupil_right.T),
        "windows": windows,
        "opening": opening.astype(np.float32),
    }


def split(values):
    high = values.astype(BF16)
    return high, (values - high.astype(F32)).astype(BF16)


def mm(a, b):
    return jnp.dot(a, b, preferred_element_type=F32)


def right(values, matrix):
    high, low = split(values)
    return mm(jnp.concatenate([high, high, low], axis=1), matrix[...])


def left(matrix, values):
    high, low = split(values)
    return mm(matrix[...], jnp.concatenate([high, high, low], axis=0))


def to_rows(spectrum):
    parts = []
    for c in range(spectrum.shape[1] // LANES):
        lanes = slice(c * LANES, (c + 1) * LANES)
        parts.append(jnp.concatenate([spectrum[:PP, lanes], spectrum[PP:, lanes]], axis=1))
    return jnp.concatenate(parts, axis=0)


def to_lanes(rows):
    count = rows.shape[0] // PP
    re = jnp.concatenate([rows[c * PP : (c + 1) * PP, :LANES] for c in range(count)], axis=1)
    im = jnp.concatenate([rows[c * PP : (c + 1) * PP, LANES:] for c in range(count)], axis=1)
    return jnp.concatenate([re, im], axis=0)


def sin_cos(angle):
    turns = jnp.floor(angle * (2.0 / math.pi) + 0.5)
    rest = angle - turns * 1.5703125
    rest = rest - turns * 4.837512969970703125e-4
    rest = rest - turns * 7.54978995489188216e-8
    sq = rest * rest
    sine = ((-1.9515295891e-4 * sq + 8.3321608736e-3) * sq - 1.6666654611e-1) * sq * rest + rest
    cosine = ((2.443315711809948e-5 * sq - 1.388731625493765e-3) * sq + 4.166664568298827e-2) * sq * sq - 0.5 * sq + 1.0
    quarter = turns.astype(jnp.int32) & 3
    swapped = (quarter & 1) == 1
    sin_now = jnp.where(swapped, cosine, sine)
    cos_now = jnp.where(swapped, sine, cosine)
    sin_now = jnp.where(quarter >= 2, -sin_now, sin_now)
    cos_now = jnp.where((quarter == 1) | (quarter == 2), -cos_now, cos_now)
    return sin_now, cos_now


def fetch(pairs, sems):
    copies = [pltpu.make_async_copy(src, dst, sems.at[i]) for i, (src, dst) in enumerate(pairs)]
    for copy in copies:
        copy.start()
    return copies


def is_early():
    return lax.axis_index("patch") % 8 == 0


def pupil_part(coeffs_hbm, opening_hbm, basis_hbm, pupil_ref, basis_scr, wave_scr, coeffs_ref, opening_ref, sems, later):
    copies = fetch(
        [(coeffs_hbm, coeffs_ref)]
        + [(basis_hbm.at[:, pl.ds(j * CHUNK, CHUNK)], basis_scr.at[j]) for j in range(CHUNKS)]
        + [(opening_hbm, opening_ref)],
        sems,
    )
    late_copies = fetch(*later)
    pupil_ref[...] = jnp.zeros_like(pupil_ref)
    copies[0].wait()
    coeffs = jnp.concatenate([coeffs_ref[0, 0], coeffs_ref[1, 0]], axis=0)
    c_high = coeffs.astype(BF16)
    rest = coeffs - c_high.astype(F32)
    c_mid = rest.astype(BF16)
    c_low = (rest - c_mid.astype(F32)).astype(BF16)
    c_all = jnp.concatenate([c_high, c_mid, c_low], axis=0)
    for j in range(CHUNKS):
        copies[1 + j].wait()
        basis = basis_scr[j]
        b_high = basis.astype(BF16)
        b_rest = basis - b_high.astype(F32)
        b_mid = b_rest.astype(BF16)
        b_low = (b_rest - b_mid.astype(F32)).astype(BF16)
        by_high, by_mid, by_low = mm(c_all, b_high), mm(c_all[: 2 * NI], b_mid), mm(c_high, b_low)
        small = by_low + by_mid[NI:] + by_high[2 * NI :]
        wave_scr[:, j * CHUNK : (j + 1) * CHUNK] = small + (by_mid[:NI] + by_high[NI : 2 * NI]) + by_high[:NI]
    copies[1 + CHUNKS].wait()
    sine, cosine = sin_cos(wave_scr[...])
    opening = opening_ref[...]
    re = cosine * opening
    im = sine * opening
    for a in range(PU):
        pupil_ref[a * NI : (a + 1) * NI, 0:PU] = re[:, a * PU : (a + 1) * PU]
        pupil_ref[a * NI : (a + 1) * NI, 64 : 64 + PU] = im[:, a * PU : (a + 1) * PU]
    for copy in late_copies:
        copy.wait()


def pack_kernel(object_hbm, data_hbm, coeffs_hbm, opening_hbm, basis_hbm, pr_hbm, pl_hbm,
                on_ref, off_ref, pupil_ref, pr_ref, pl_ref, on_scr, off_scr, send_sems, matrix_sems, *scratch):
    even = lax.axis_index("patch") % 2 == 0
    low, high = STRIDE - HALO, 0
    on_at = pl.multiple_of(jnp.where(even, low, high), 8)
    off_at = pl.multiple_of(jnp.where(even, high, low), 8)
    copies = fetch(
        [
            (object_hbm.at[pl.ds(off_at, HALO)], off_ref.at[pl.ds(0, HALO)]),
            (data_hbm.at[pl.ds(off_at, HALO)], off_scr),
            (object_hbm.at[pl.ds(on_at, HALO)], on_ref.at[pl.ds(0, HALO)]),
            (data_hbm.at[pl.ds(on_at, HALO)], on_scr),
        ],
        send_sems,
    )

    @pl.when(is_early())
    def _():
        matrices = [(pr_hbm, pr_ref), (pl_hbm, pl_ref)]
        pupil_part(coeffs_hbm, opening_hbm, basis_hbm, pupil_ref, *scratch, (matrices, matrix_sems))

    for copy in copies:
        copy.wait()
    for k in range(FK):
        rows = slice((k + 1) * HALO, (k + 2) * HALO)
        off_ref[rows, :] = off_scr[:, k, :]
        on_ref[rows, :] = on_scr[:, k, :]


def psf_kernel(pupil_in, pr_in, pl_in, coeffs_hbm, opening_hbm, basis_hbm, object_hbm, data_hbm, pr_hbm, pl_hbm, fl_hbm, fr_hbm,
               windows_hbm, rl_hbm, bl_hbm, br_hbm,
               pupil_ref, pr_ref, pl_ref, fl_ref, fr_ref, field_ref, spec_ref, scale_ref, ext, windows_ref, rl_ref, bl_ref, br_ref,
               rows_scr, left_scr, data_scr, sems, matrix_sems, *scratch):
    copies = fetch(
        [
            (fl_hbm, fl_ref), (fr_hbm, fr_ref),
            (object_hbm, ext.at[0, pl.ds(HALO, STRIDE), pl.ds(LANES, 2 * LANES)]),
            (data_hbm, data_scr), (windows_hbm, windows_ref), (rl_hbm, rl_ref), (bl_hbm, bl_ref), (br_hbm, br_ref),
        ],
        sems,
    )
    for i in range(1 + FK):
        ext[i, :, 0:LANES] = jnp.zeros((HEIGHT, LANES), F32)
        ext[i, :, 3 * LANES :] = jnp.zeros((HEIGHT, LANES), F32)
        ext[i, STRIDE + 2 * HALO :, LANES : 3 * LANES] = jnp.zeros((HEIGHT - STRIDE - 2 * HALO, 2 * LANES), F32)
    @pl.when(jnp.logical_not(is_early()))
    def _():
        matrices = [(pr_hbm, pr_ref), (pl_hbm, pl_ref)]
        pupil_part(coeffs_hbm, opening_hbm, basis_hbm, pupil_ref, *scratch, (matrices, matrix_sems))

    mixed = right(pupil_ref[...], pr_ref)
    rows_scr[0] = mixed[:, :LANES]
    rows_scr[1] = mixed[:, LANES:]
    for n in range(NI):
        lanes = slice(n * LANES, (n + 1) * LANES)
        left_scr[0:PU, lanes] = rows_scr[0, pl.ds(n, PU, stride=NI), :]
        left_scr[PU:, lanes] = rows_scr[1, pl.ds(n, PU, stride=NI), :]
    field = left(pl_ref, left_scr[...])
    field_ref[...] = field
    intensity = field[:PP] * field[:PP] + field[PP:] * field[PP:]
    sums = jnp.concatenate(
        [jnp.sum(intensity[:, n * LANES : (n + 1) * LANES], axis=0, keepdims=True) for n in range(NI)], axis=0
    )
    scale = 1.0 / jnp.sum(sums, axis=1, keepdims=True)
    scale_ref[...] = jnp.broadcast_to(scale, (NI, LANES))
    spread = jnp.concatenate(
        [intensity[:, n * LANES : (n + 1) * LANES] * scale[n : n + 1, :] for n in range(NI)], axis=1
    )
    pair = jnp.concatenate([spread[:, : PC * LANES], spread[:, PC * LANES :]], axis=0)
    copies[0].wait()
    copies[1].wait()
    half = PC // 2 * LANES
    mixed = [left(fl_ref, pair[:, g * half : (g + 1) * half]) for g in range(2)]
    spectra = [right(to_rows(values), fr_ref) for values in mixed]
    spec_ref[...] = jnp.concatenate(spectra, axis=0)
    for copy in copies[2:]:
        copy.wait()
    for k in range(FK):
        ext[k + 1, HALO : HALO + STRIDE, LANES : 3 * LANES] = data_scr[:, k, :]


def misfit_kernel(offsets_ref, kinds_ref, counts_ref, off_ref, on_ref, spec_ref, ext_in, windows_ref, rl_ref, fl_ref, fr_ref,
                  obj_spec_ref, res_spec_ref, centre_ref, on_rim_ref, off_rim_ref, ext, total):
    even = lax.axis_index("patch") % 2 == 0
    on_at = pl.multiple_of(jnp.where(even, STRIDE + HALO, 0), 8)
    off_at = pl.multiple_of(jnp.where(even, 0, STRIDE + HALO), 8)
    mid = slice(LANES, 3 * LANES)
    total[...] = jnp.zeros_like(total)
    for i in range(1 + FK):
        ext[i] = ext_in[i]
        ext[i, pl.ds(on_at, HALO), mid] = on_ref[i * HALO : (i + 1) * HALO, :]
        ext[i, pl.ds(off_at, HALO), mid] = off_ref[i * HALO : (i + 1) * HALO, :]

    row_base = [pl.multiple_of((offsets_ref[0, 0, c] >> 3) << 3, 8) for c in range(PC)]
    row_rest = [offsets_ref[0, 0, c] & 7 for c in range(PC)]
    base = [0, LANES, LANES, 2 * LANES]
    shift = [LANES + c * STRIDE - HALO - base[c] + offsets_ref[0, 1, c] for c in range(PC)]

    def cut(i, c):
        block = ext[i, pl.ds(row_base[c], TALL), base[c] : base[c] + 2 * LANES]
        moved = pltpu.roll(block, 2 * LANES - shift[c], 1)[:, :LANES]
        return pltpu.roll(moved, jnp.where(row_rest[c] == 0, 0, TALL - row_rest[c]), 0)[:PP]

    pairs = [(0, 1), (2, 3)]
    windows = [windows_ref[kinds_ref[0, c]] for c in range(PC)]
    weighted = [jnp.concatenate([windows[c] * cut(0, c) for c in pair], axis=1) for pair in pairs]
    taken = [
        jnp.concatenate([jnp.concatenate([windows[c] * cut(k + 1, c) for c in pair], axis=1) for k in range(FK)], axis=0)
        for pair in pairs
    ]
    obj_left = [left(rl_ref, values) for values in weighted]
    data_left = [left(fl_ref, values) for values in taken]
    obj = [right(to_rows(values), fr_ref) for values in obj_left]
    data = [right(to_rows(values), fr_ref) for values in data_left]
    back = []
    for g, pair in enumerate(pairs):
        rows = slice(pair[0] * PP, (pair[-1] + 1) * PP)
        obj_spec_ref[rows, :] = obj[g]
        o_re, o_im, s_re, s_im = obj[g][:, :LANES], obj[g][:, LANES:], spec_ref[rows, :LANES], spec_ref[rows, LANES:]
        product = jnp.concatenate([o_re * s_re - o_im * s_im, o_re * s_im + o_im * s_re], axis=1)
        usable = [jnp.where(c < counts_ref[0, 0], 1.0, 0.0).astype(F32) for c in pair]
        difference = product - data[g]
        res = jnp.concatenate([difference[i * PP : (i + 1) * PP] * usable[i] for i in range(len(pair))], axis=0)
        res_spec_ref[rows, :] = res
        r_re, r_im = res[:, :LANES], res[:, LANES:]
        back.append(jnp.concatenate([s_re * r_re + s_im * r_im, s_im * r_re - s_re * r_im], axis=1))
    mixed = [to_lanes(right(values, fr_ref)) for values in back]
    grad = jnp.concatenate([left(fl_ref[:PP, :], values) for values in mixed], axis=1)
    for c in range(PC):
        mine = windows[c] * grad[:, c * LANES : (c + 1) * LANES] * (1.0 / (PP * PP))
        mine = pltpu.roll(jnp.concatenate([mine, jnp.zeros((TALL - PP, LANES), F32)], axis=0), row_rest[c], 0)
        placed = pltpu.roll(jnp.concatenate([mine, jnp.zeros((TALL, LANES), F32)], axis=1), shift[c], 1)
        rows, lanes = pl.ds(row_base[c], TALL), slice(base[c], base[c] + 2 * LANES)
        total[rows, lanes] = total[rows, lanes] + placed
    centre_ref[...] = total[HALO : HALO + STRIDE, mid]
    on_rim_ref[...] = total[pl.ds(on_at, HALO), mid]
    off_rim_ref[...] = total[pl.ds(off_at, HALO), mid]


def spread_grad_kernel(obj_spec_ref, res_spec_ref, fl_ref, fr_ref, grad_ref):
    obj, res = obj_spec_ref[...], res_spec_ref[...]
    o_re, o_im, r_re, r_im = obj[:, :LANES], obj[:, LANES:], res[:, :LANES], res[:, LANES:]
    back = jnp.concatenate([o_re * r_re + o_im * r_im, o_im * r_re - o_re * r_im], axis=1)
    grad_ref[...] = left(fl_ref, to_lanes(right(back, fr_ref)))


def phase_grad_kernel(grad_ref, field_ref, scale_ref, pupil_ref, bl_ref, br_ref, basis_hbm, flat_ref, basis_ref, rows_scr, sems):
    copies = fetch([(basis_hbm, basis_ref)], sems)
    re_parts, im_parts = [], []
    for n in range(NI):
        k, c = divmod(n, PC)
        lanes = slice(n * LANES, (n + 1) * LANES)
        f_re, f_im = field_ref[:PP, lanes], field_ref[PP:, lanes]
        scale = scale_ref[n : n + 1, :]
        spread = (f_re * f_re + f_im * f_im) * scale
        mine = grad_ref[k * PP : (k + 1) * PP, c * LANES : (c + 1) * LANES] * ((1 - 2 * k) / (PP * PP))
        mean = jnp.sum(jnp.sum(mine * spread, axis=0, keepdims=True), axis=1, keepdims=True)
        slope = 2.0 * scale * (mine - mean)
        re_parts.append(f_re * slope)
        im_parts.append(f_im * slope)
    wide = jnp.concatenate([jnp.concatenate(re_parts, axis=1), jnp.concatenate(im_parts, axis=1)], axis=0)
    half = left(bl_ref, wide)
    for n in range(NI):
        lanes = slice(n * LANES, (n + 1) * LANES)
        rows_scr[0, pl.ds(n, PU, stride=NI), :] = half[:PU, lanes]
        rows_scr[1, pl.ds(n, PU, stride=NI), :] = half[PU:, lanes]
    pupil_grad = right(jnp.concatenate([rows_scr[0], rows_scr[1]], axis=1), br_ref)
    pupil = pupil_ref[...]
    crossed = pupil * pltpu.roll(pupil_grad, 64, 1)
    slopes = crossed - pltpu.roll(crossed, 64, 1)
    for a in range(PU):
        flat_ref[:, a * PU : (a + 1) * PU] = slopes[a * NI : (a + 1) * NI, 0:PU]
    copies[0].wait()


def mode_kernel(flat_ref, basis_ref, out_ref):
    high, low = split(flat_ref[...])
    b_high, b_low = split(basis_ref[...])

    def by_modes(a, b):
        return lax.dot_general(a, b, (((1,), (1,)), ((), ())), preferred_element_type=F32)

    first = by_modes(jnp.concatenate([high, low], axis=0), b_high)
    out = first[:NI] + first[NI:] + by_modes(high, b_low)
    out_ref[0, 0] = out[:PC]
    out_ref[1, 0] = out[PC:]


def call(kernel, out_shapes, scratch=(), smem=0, near=0, far=0, aliases=None, name=None):
    vmem = pl.BlockSpec(memory_space=pltpu.VMEM)
    inner = pl.pallas_call(
        kernel,
        out_shape=out_shapes,
        in_specs=[pl.BlockSpec(memory_space=pltpu.SMEM)] * smem + [vmem] * near + [pl.BlockSpec(memory_space=pltpu.HBM)] * far,
        out_specs=jax.tree.map(lambda _: vmem, out_shapes),
        scratch_shapes=list(scratch),
        input_output_aliases=aliases or {},
        compiler_params=pltpu.CompilerParams(vmem_limit_bytes=VMEM_LIMIT),
        name=name,
    )

    def run(*operands):
        placed = list(operands)
        for i in range(smem + near, smem + near + far):
            placed[i] = pltpu.with_memory_space_constraint(placed[i], pltpu.HBM)
        for i in range(smem, smem + near):
            placed[i] = pltpu.with_memory_space_constraint(placed[i], pltpu.VMEM)
        return inner(*placed)

    return run


def shape(*dims):
    return pltpu.VMEM(dims, F32)


def sems(count):
    return pltpu.SemaphoreType.DMA((count,))


def like(value):
    return pltpu.VMEM(value.shape, BF16 if value.dtype == ml_dtypes.bfloat16 else F32)


def swap_on(values):
    count = lax.axis_size("patch")
    return lax.ppermute(values, "patch", [(i, i ^ 1) for i in range(count)])


def swap_off(values):
    count = lax.axis_size("patch")
    pairs = [(i, i + 1) for i in range(1, count - 1, 2)]
    return lax.ppermute(values, "patch", pairs + [(j, i) for i, j in pairs])


def swap_frames(values, bit):
    count = lax.axis_size("frames")
    return lax.ppermute(values, "frames", [(i, i ^ bit) for i in range(count)])


def body(object_band, data_band, coeffs, mode_basis, offsets, window_ids, counts):
    columns = object_band.shape[1]
    host = constants()
    const = {name: jnp.asarray(value) for name, value in host.items()}
    room = {name: like(value) for name, value in host.items()}
    halo_room = pltpu.VMEM((HALO, FK, columns), F32)
    pupil_room = [
        pltpu.VMEM((CHUNKS, MODES, CHUNK), F32), pltpu.VMEM((NI, PU * PU), F32), pltpu.VMEM((FK, 1, PC, MODES), F32),
        room["opening"], sems(CHUNKS + 2),
    ]
    wave_given = (coeffs, const["opening"], mode_basis)
    early_matrices = ("pupil_right", "pupil_left", "fwd_left", "fwd_right")
    matrices = [const[name] for name in early_matrices]
    made_early = [shape(PU * NI, LANES)] + [room[name] for name in early_matrices[:2]]
    on_send, off_send, *early = call(
        pack_kernel, [shape(3 * HALO, columns)] * 2 + made_early,
        scratch=[halo_room, halo_room, sems(4), sems(4)] + pupil_room, far=7, name="pack",
    )(object_band, data_band, *wave_given, *matrices[:2])
    on_halo = swap_on(on_send)
    off_halo = swap_off(off_send)
    kept = ("windows", "real_left", "back_left", "back_right")
    pupil, _, _, fwd_left, fwd_right, field, spec, scale, ext, *kept_values = call(
        psf_kernel,
        made_early + [room[name] for name in early_matrices[2:]] + [shape(2 * PP, NI * LANES), shape(PC * PP, 2 * LANES), shape(NI, LANES), shape(1 + FK, HEIGHT, 4 * LANES)]
        + [room[name] for name in kept],
        scratch=[
            pltpu.VMEM((2, PU * NI, LANES), F32), pltpu.VMEM((2 * PU, NI * LANES), F32), pltpu.VMEM((STRIDE, FK, columns), F32),
            sems(8), sems(4),
        ] + pupil_room,
        near=3,
        far=13,
        aliases={i: i for i in range(3)},
        name="psf",
    )(*early, *wave_given, object_band, data_band, *matrices, *[const[name] for name in kept])
    here = dict(zip(kept, kept_values))
    obj_spec, res_spec, centre, on_rim, off_rim = call(
        misfit_kernel,
        [shape(PC * PP, 2 * LANES)] * 2 + [shape(STRIDE, columns), shape(HALO, columns), shape(HALO, columns)],
        scratch=[pltpu.VMEM((1 + FK, HEIGHT, 4 * LANES), F32), pltpu.VMEM((HEIGHT, 4 * LANES), F32)],
        smem=3,
        near=8,
        name="misfit",
    )(
        jnp.transpose(offsets, (0, 2, 1)), window_ids, counts.reshape(1, 1), off_halo, on_halo, spec, ext,
        here["windows"], here["real_left"], fwd_left, fwd_right,
    )
    on_rim = swap_on(on_rim)
    off_rim = swap_off(off_rim)
    spread_grad = call(spread_grad_kernel, shape(2 * PP, PC * LANES), near=4, name="spread_grad")(
        obj_spec, res_spec, fwd_left, fwd_right
    )
    even = lax.axis_index("patch") % 2 == 0
    upper = jnp.where(even, off_rim, on_rim)
    lower = jnp.where(even, on_rim, off_rim)
    rows = jnp.concatenate([centre[:HALO] + upper, centre[HALO : STRIDE - HALO], centre[STRIDE - HALO :] + lower], axis=0)
    rows, spread_grad = lax.optimization_barrier((rows, spread_grad))
    moved = swap_frames(rows, 5) + swap_frames(rows, 4) + swap_frames(rows, 1)
    flat, basis = call(
        phase_grad_kernel, [shape(NI, PU * PU), shape(*mode_basis.shape)],
        scratch=[pltpu.VMEM((2, PU * NI, LANES), F32), sems(1)], near=6, far=1, name="phase_grad",
    )(spread_grad, field, scale, pupil, here["back_left"], here["back_right"], mode_basis)
    rows = rows + moved
    rows, flat = lax.optimization_barrier((rows, flat))
    coeff_grad = call(mode_kernel, jax.ShapeDtypeStruct((FK, 1, PC, MODES), F32), near=2, name="modes")(flat, basis)
    rows = rows + swap_frames(rows, 3)
    return rows, coeff_grad


def solution(mesh):
    in_specs = (
        P("patch", None),
        P("patch", "frames", None),
        P("frames", "patch", None, None),
        P(),
        P("patch", None, None),
        P("patch", None),
        P("patch"),
    )
    out_specs = (P("patch", None), P("frames", "patch", None, None))
    return jax.shard_map(body, mesh=mesh, in_specs=in_specs, out_specs=out_specs, check_vma=False)
```

```python
import math

import jax
import jax.numpy as jnp
import ml_dtypes
import numpy as np
from jax import lax
from jax.experimental import pallas as pl
from jax.experimental.pallas import tpu as pltpu
from jax.sharding import PartitionSpec as P

PP = 96
PU = 48
STRIDE = 64
HALO = 24
PC = 4
FK = 2
NI = PC * FK
LANES = 128
MODES = 200
TALL = PP + 8
HEIGHT = STRIDE + 2 * HALO + 8
F32 = jnp.float32
BF16 = jnp.bfloat16
VMEM_LIMIT = 16 * 1024 * 1024
CHUNK = 768
CHUNKS = PU * PU // CHUNK


def halves(matrix):
    high = matrix.astype(ml_dtypes.bfloat16)
    low = (matrix - high.astype(np.float64)).astype(ml_dtypes.bfloat16)
    return high, low


def dft(points, length):
    turns = np.outer(np.arange(points), np.arange(length)) % points
    angles = 2.0 * math.pi / points * turns
    return np.cos(angles), -np.sin(angles)


def constants():
    full_re, full_im = dft(PP, PP)
    half_re, half_im = dft(PP, PU)
    fwd_right = np.zeros((256, 256))
    fwd_right[:96, :96] = full_re
    fwd_right[128:224, :96] = -full_im
    fwd_right[:96, 128:224] = full_im
    fwd_right[128:224, 128:224] = full_re
    pupil_right = np.zeros((128, 256))
    pupil_right[:48, :96] = half_re.T
    pupil_right[64:112, :96] = -half_im.T
    pupil_right[:48, 128:224] = half_im.T
    pupil_right[64:112, 128:224] = half_re.T
    pupil_left = np.block([[half_re, -half_im], [half_im, half_re]])
    fwd_left = np.block([[full_re, -full_im], [full_im, full_re]])
    real_left = np.concatenate([full_re, full_im], axis=0)

    def tall(matrix):
        high, low = halves(matrix)
        return np.concatenate([high, low, high], axis=0)

    def wide(matrix):
        high, low = halves(matrix)
        return np.concatenate([high, low, high], axis=1)

    side = np.arange(PP) + 0.5
    windows = np.zeros((4, PP, LANES), np.float32)
    for kind in range(4):
        edge = float(max(PP * (kind + 1) // 12, 1))
        rising = 0.5 - 0.5 * np.cos(math.pi * np.minimum(side, edge) / edge)
        profile = rising * rising[::-1]
        windows[kind, :, :PP] = np.outer(profile, profile)
    centre = np.arange(PU) + 0.5 - 0.5 * PU
    opening = (centre[:, None] ** 2 + centre[None, :] ** 2 <= (0.5 * PU) ** 2).reshape(1, PU * PU)
    return {
        "fwd_right": tall(fwd_right),
        "pupil_right": tall(pupil_right),
        "pupil_left": wide(pupil_left),
        "fwd_left": wide(fwd_left),
        "real_left": wide(real_left),
        "back_left": wide(pupil_left.T),
        "back_right": tall(pupil_right.T),
        "windows": windows,
        "opening": opening.astype(np.float32),
    }


def split(values):
    high = values.astype(BF16)
    return high, (values - high.astype(F32)).astype(BF16)


def mm(a, b):
    return jnp.dot(a, b, preferred_element_type=F32)


def right(values, matrix):
    high, low = split(values)
    return mm(jnp.concatenate([high, high, low], axis=1), matrix[...])


def left(matrix, values):
    high, low = split(values)
    return mm(matrix[...], jnp.concatenate([high, high, low], axis=0))


def to_rows(spectrum):
    parts = []
    for c in range(spectrum.shape[1] // LANES):
        lanes = slice(c * LANES, (c + 1) * LANES)
        parts.append(jnp.concatenate([spectrum[:PP, lanes], spectrum[PP:, lanes]], axis=1))
    return jnp.concatenate(parts, axis=0)


def to_lanes(rows):
    count = rows.shape[0] // PP
    re = jnp.concatenate([rows[c * PP : (c + 1) * PP, :LANES] for c in range(count)], axis=1)
    im = jnp.concatenate([rows[c * PP : (c + 1) * PP, LANES:] for c in range(count)], axis=1)
    return jnp.concatenate([re, im], axis=0)


def sin_cos(angle):
    turns = jnp.floor(angle * (2.0 / math.pi) + 0.5)
    rest = angle - turns * 1.5703125
    rest = rest - turns * 4.837512969970703125e-4
    rest = rest - turns * 7.54978995489188216e-8
    sq = rest * rest
    sine = ((-1.9515295891e-4 * sq + 8.3321608736e-3) * sq - 1.6666654611e-1) * sq * rest + rest
    cosine = ((2.443315711809948e-5 * sq - 1.388731625493765e-3) * sq + 4.166664568298827e-2) * sq * sq - 0.5 * sq + 1.0
    quarter = turns.astype(jnp.int32) & 3
    swapped = (quarter & 1) == 1
    sin_now = jnp.where(swapped, cosine, sine)
    cos_now = jnp.where(swapped, sine, cosine)
    sin_now = jnp.where(quarter >= 2, -sin_now, sin_now)
    cos_now = jnp.where((quarter == 1) | (quarter == 2), -cos_now, cos_now)
    return sin_now, cos_now


def fetch(pairs, sems):
    copies = [pltpu.make_async_copy(src, dst, sems.at[i]) for i, (src, dst) in enumerate(pairs)]
    for copy in copies:
        copy.start()
    return copies


def is_early():
    return lax.axis_index("patch") % 8 == 0


def pupil_part(coeffs_hbm, opening_hbm, basis_hbm, pupil_ref, basis_scr, wave_scr, coeffs_ref, opening_ref, sems, later):
    copies = fetch(
        [(coeffs_hbm, coeffs_ref)]
        + [(basis_hbm.at[:, pl.ds(j * CHUNK, CHUNK)], basis_scr.at[j]) for j in range(CHUNKS)]
        + [(opening_hbm, opening_ref)],
        sems,
    )
    late_copies = fetch(*later)
    pupil_ref[...] = jnp.zeros_like(pupil_ref)
    copies[0].wait()
    coeffs = jnp.concatenate([coeffs_ref[0, 0], coeffs_ref[1, 0]], axis=0)
    c_high = coeffs.astype(BF16)
    rest = coeffs - c_high.astype(F32)
    c_mid = rest.astype(BF16)
    c_low = (rest - c_mid.astype(F32)).astype(BF16)
    c_all = jnp.concatenate([c_high, c_mid, c_low], axis=0)
    for j in range(CHUNKS):
        copies[1 + j].wait()
        basis = basis_scr[j]
        b_high = basis.astype(BF16)
        b_rest = basis - b_high.astype(F32)
        b_mid = b_rest.astype(BF16)
        b_low = (b_rest - b_mid.astype(F32)).astype(BF16)
        by_high, by_mid, by_low = mm(c_all, b_high), mm(c_all[: 2 * NI], b_mid), mm(c_high, b_low)
        small = by_low + by_mid[NI:] + by_high[2 * NI :]
        wave_scr[:, j * CHUNK : (j + 1) * CHUNK] = small + (by_mid[:NI] + by_high[NI : 2 * NI]) + by_high[:NI]
    copies[1 + CHUNKS].wait()
    sine, cosine = sin_cos(wave_scr[...])
    opening = opening_ref[...]
    re = cosine * opening
    im = sine * opening
    for a in range(PU):
        pupil_ref[a * NI : (a + 1) * NI, 0:PU] = re[:, a * PU : (a + 1) * PU]
        pupil_ref[a * NI : (a + 1) * NI, 64 : 64 + PU] = im[:, a * PU : (a + 1) * PU]
    for copy in late_copies:
        copy.wait()


def pack_kernel(object_hbm, data_hbm, coeffs_hbm, opening_hbm, basis_hbm, pr_hbm, pl_hbm,
                on_ref, off_ref, pupil_ref, pr_ref, pl_ref, on_scr, off_scr, send_sems, matrix_sems, *scratch):
    even = lax.axis_index("patch") % 2 == 0
    low, high = STRIDE - HALO, 0
    on_at = pl.multiple_of(jnp.where(even, low, high), 8)
    off_at = pl.multiple_of(jnp.where(even, high, low), 8)
    copies = fetch(
        [
            (object_hbm.at[pl.ds(off_at, HALO)], off_ref.at[pl.ds(0, HALO)]),
            (data_hbm.at[pl.ds(off_at, HALO)], off_scr),
            (object_hbm.at[pl.ds(on_at, HALO)], on_ref.at[pl.ds(0, HALO)]),
            (data_hbm.at[pl.ds(on_at, HALO)], on_scr),
        ],
        send_sems,
    )

    @pl.when(is_early())
    def _():
        matrices = [(pr_hbm, pr_ref), (pl_hbm, pl_ref)]
        pupil_part(coeffs_hbm, opening_hbm, basis_hbm, pupil_ref, *scratch, (matrices, matrix_sems))

    for copy in copies:
        copy.wait()
    for k in range(FK):
        rows = slice((k + 1) * HALO, (k + 2) * HALO)
        off_ref[rows, :] = off_scr[:, k, :]
        on_ref[rows, :] = on_scr[:, k, :]


def psf_kernel(pupil_in, pr_in, pl_in, coeffs_hbm, opening_hbm, basis_hbm, object_hbm, data_hbm, pr_hbm, pl_hbm, fl_hbm, fr_hbm,
               windows_hbm, rl_hbm, bl_hbm, br_hbm,
               pupil_ref, pr_ref, pl_ref, fl_ref, fr_ref, field_ref, spec_ref, scale_ref, ext, windows_ref, rl_ref, bl_ref, br_ref,
               rows_scr, left_scr, data_scr, sems, matrix_sems, *scratch):
    copies = fetch(
        [
            (fl_hbm, fl_ref), (fr_hbm, fr_ref),
            (object_hbm, ext.at[0, pl.ds(HALO, STRIDE), pl.ds(LANES, 2 * LANES)]),
            (data_hbm, data_scr), (windows_hbm, windows_ref), (rl_hbm, rl_ref), (bl_hbm, bl_ref), (br_hbm, br_ref),
        ],
        sems,
    )
    for i in range(1 + FK):
        ext[i, :, 0:LANES] = jnp.zeros((HEIGHT, LANES), F32)
        ext[i, :, 3 * LANES :] = jnp.zeros((HEIGHT, LANES), F32)
        ext[i, STRIDE + 2 * HALO :, LANES : 3 * LANES] = jnp.zeros((HEIGHT - STRIDE - 2 * HALO, 2 * LANES), F32)
    @pl.when(jnp.logical_not(is_early()))
    def _():
        matrices = [(pr_hbm, pr_ref), (pl_hbm, pl_ref)]
        pupil_part(coeffs_hbm, opening_hbm, basis_hbm, pupil_ref, *scratch, (matrices, matrix_sems))

    mixed = right(pupil_ref[...], pr_ref)
    rows_scr[0] = mixed[:, :LANES]
    rows_scr[1] = mixed[:, LANES:]
    for n in range(NI):
        lanes = slice(n * LANES, (n + 1) * LANES)
        left_scr[0:PU, lanes] = rows_scr[0, pl.ds(n, PU, stride=NI), :]
        left_scr[PU:, lanes] = rows_scr[1, pl.ds(n, PU, stride=NI), :]
    count = NI // 2 * LANES
    field = jnp.concatenate([left(pl_ref, left_scr[:, g * count : (g + 1) * count]) for g in range(2)], axis=1)
    field_ref[...] = field
    intensity = field[:PP] * field[:PP] + field[PP:] * field[PP:]
    sums = jnp.concatenate(
        [jnp.sum(intensity[:, n * LANES : (n + 1) * LANES], axis=0, keepdims=True) for n in range(NI)], axis=0
    )
    scale = 1.0 / jnp.sum(sums, axis=1, keepdims=True)
    scale_ref[...] = jnp.broadcast_to(scale, (NI, LANES))
    spread = jnp.concatenate(
        [intensity[:, n * LANES : (n + 1) * LANES] * scale[n : n + 1, :] for n in range(NI)], axis=1
    )
    pair = jnp.concatenate([spread[:, : PC * LANES], spread[:, PC * LANES :]], axis=0)
    copies[0].wait()
    copies[1].wait()
    half = PC // 2 * LANES
    mixed = [left(fl_ref, pair[:, g * half : (g + 1) * half]) for g in range(2)]
    spectra = [right(to_rows(values), fr_ref) for values in mixed]
    spec_ref[...] = jnp.concatenate(spectra, axis=0)
    for copy in copies[2:]:
        copy.wait()
    for k in range(FK):
        ext[k + 1, HALO : HALO + STRIDE, LANES : 3 * LANES] = data_scr[:, k, :]


def misfit_kernel(offsets_ref, kinds_ref, counts_ref, off_ref, on_ref, spec_ref, ext_in, windows_ref, rl_ref, fl_ref, fr_ref,
                  obj_spec_ref, res_spec_ref, centre_ref, on_rim_ref, off_rim_ref, ext, total):
    even = lax.axis_index("patch") % 2 == 0
    on_at = pl.multiple_of(jnp.where(even, STRIDE + HALO, 0), 8)
    off_at = pl.multiple_of(jnp.where(even, 0, STRIDE + HALO), 8)
    mid = slice(LANES, 3 * LANES)
    total[...] = jnp.zeros_like(total)
    for i in range(1 + FK):
        ext[i] = ext_in[i]
        ext[i, pl.ds(on_at, HALO), mid] = on_ref[i * HALO : (i + 1) * HALO, :]
        ext[i, pl.ds(off_at, HALO), mid] = off_ref[i * HALO : (i + 1) * HALO, :]

    row_base = [pl.multiple_of((offsets_ref[0, 0, c] >> 3) << 3, 8) for c in range(PC)]
    row_rest = [offsets_ref[0, 0, c] & 7 for c in range(PC)]
    base = [0, LANES, LANES, 2 * LANES]
    shift = [LANES + c * STRIDE - HALO - base[c] + offsets_ref[0, 1, c] for c in range(PC)]

    def cut(i, c):
        block = ext[i, pl.ds(row_base[c], TALL), base[c] : base[c] + 2 * LANES]
        moved = pltpu.roll(block, 2 * LANES - shift[c], 1)[:, :LANES]
        return pltpu.roll(moved, jnp.where(row_rest[c] == 0, 0, TALL - row_rest[c]), 0)[:PP]

    pairs = [(0, 1), (2, 3)]
    windows = [windows_ref[kinds_ref[0, c]] for c in range(PC)]
    weighted = [jnp.concatenate([windows[c] * cut(0, c) for c in pair], axis=1) for pair in pairs]
    taken = [
        jnp.concatenate([jnp.concatenate([windows[c] * cut(k + 1, c) for c in pair], axis=1) for k in range(FK)], axis=0)
        for pair in pairs
    ]
    obj_left = [left(rl_ref, values) for values in weighted]
    data_left = [left(fl_ref, values) for values in taken]
    obj = [right(to_rows(values), fr_ref) for values in obj_left]
    data = [right(to_rows(values), fr_ref) for values in data_left]
    back = []
    for g, pair in enumerate(pairs):
        rows = slice(pair[0] * PP, (pair[-1] + 1) * PP)
        obj_spec_ref[rows, :] = obj[g]
        o_re, o_im, s_re, s_im = obj[g][:, :LANES], obj[g][:, LANES:], spec_ref[rows, :LANES], spec_ref[rows, LANES:]
        product = jnp.concatenate([o_re * s_re - o_im * s_im, o_re * s_im + o_im * s_re], axis=1)
        usable = [jnp.where(c < counts_ref[0, 0], 1.0, 0.0).astype(F32) for c in pair]
        difference = product - data[g]
        res = jnp.concatenate([difference[i * PP : (i + 1) * PP] * usable[i] for i in range(len(pair))], axis=0)
        res_spec_ref[rows, :] = res
        r_re, r_im = res[:, :LANES], res[:, LANES:]
        back.append(jnp.concatenate([s_re * r_re + s_im * r_im, s_im * r_re - s_re * r_im], axis=1))
    mixed = [to_lanes(right(values, fr_ref)) for values in back]
    grad = jnp.concatenate([left(fl_ref[:PP, :], values) for values in mixed], axis=1)
    for c in range(PC):
        mine = windows[c] * grad[:, c * LANES : (c + 1) * LANES] * (1.0 / (PP * PP))
        mine = pltpu.roll(jnp.concatenate([mine, jnp.zeros((TALL - PP, LANES), F32)], axis=0), row_rest[c], 0)
        placed = pltpu.roll(jnp.concatenate([mine, jnp.zeros((TALL, LANES), F32)], axis=1), shift[c], 1)
        rows, lanes = pl.ds(row_base[c], TALL), slice(base[c], base[c] + 2 * LANES)
        total[rows, lanes] = total[rows, lanes] + placed
    centre_ref[...] = total[HALO : HALO + STRIDE, mid]
    on_rim_ref[...] = total[pl.ds(on_at, HALO), mid]
    off_rim_ref[...] = total[pl.ds(off_at, HALO), mid]


def spread_grad_kernel(obj_spec_ref, res_spec_ref, fl_ref, fr_ref, grad_ref):
    obj, res = obj_spec_ref[...], res_spec_ref[...]
    o_re, o_im, r_re, r_im = obj[:, :LANES], obj[:, LANES:], res[:, :LANES], res[:, LANES:]
    back = jnp.concatenate([o_re * r_re + o_im * r_im, o_im * r_re - o_re * r_im], axis=1)
    grad_ref[...] = left(fl_ref, to_lanes(right(back, fr_ref)))


def phase_grad_kernel(grad_ref, field_ref, scale_ref, pupil_ref, bl_ref, br_ref, basis_hbm, flat_ref, basis_ref, rows_scr, sems):
    copies = fetch([(basis_hbm, basis_ref)], sems)
    re_parts, im_parts = [], []
    for n in range(NI):
        k, c = divmod(n, PC)
        lanes = slice(n * LANES, (n + 1) * LANES)
        f_re, f_im = field_ref[:PP, lanes], field_ref[PP:, lanes]
        scale = scale_ref[n : n + 1, :]
        spread = (f_re * f_re + f_im * f_im) * scale
        mine = grad_ref[k * PP : (k + 1) * PP, c * LANES : (c + 1) * LANES] * ((1 - 2 * k) / (PP * PP))
        mean = jnp.sum(jnp.sum(mine * spread, axis=0, keepdims=True), axis=1, keepdims=True)
        slope = 2.0 * scale * (mine - mean)
        re_parts.append(f_re * slope)
        im_parts.append(f_im * slope)
    wide = jnp.concatenate([jnp.concatenate(re_parts, axis=1), jnp.concatenate(im_parts, axis=1)], axis=0)
    half = left(bl_ref, wide)
    for n in range(NI):
        lanes = slice(n * LANES, (n + 1) * LANES)
        rows_scr[0, pl.ds(n, PU, stride=NI), :] = half[:PU, lanes]
        rows_scr[1, pl.ds(n, PU, stride=NI), :] = half[PU:, lanes]
    pupil_grad = right(jnp.concatenate([rows_scr[0], rows_scr[1]], axis=1), br_ref)
    pupil = pupil_ref[...]
    crossed = pupil * pltpu.roll(pupil_grad, 64, 1)
    slopes = crossed - pltpu.roll(crossed, 64, 1)
    for a in range(PU):
        flat_ref[:, a * PU : (a + 1) * PU] = slopes[a * NI : (a + 1) * NI, 0:PU]
    copies[0].wait()


def mode_kernel(flat_ref, basis_ref, out_ref):
    high, low = split(flat_ref[...])
    b_high, b_low = split(basis_ref[...])

    def by_modes(a, b):
        return lax.dot_general(a, b, (((1,), (1,)), ((), ())), preferred_element_type=F32)

    first = by_modes(jnp.concatenate([high, low], axis=0), b_high)
    out = first[:NI] + first[NI:] + by_modes(high, b_low)
    out_ref[0, 0] = out[:PC]
    out_ref[1, 0] = out[PC:]


def call(kernel, out_shapes, scratch=(), smem=0, near=0, far=0, aliases=None, name=None):
    vmem = pl.BlockSpec(memory_space=pltpu.VMEM)
    inner = pl.pallas_call(
        kernel,
        out_shape=out_shapes,
        in_specs=[pl.BlockSpec(memory_space=pltpu.SMEM)] * smem + [vmem] * near + [pl.BlockSpec(memory_space=pltpu.HBM)] * far,
        out_specs=jax.tree.map(lambda _: vmem, out_shapes),
        scratch_shapes=list(scratch),
        input_output_aliases=aliases or {},
        compiler_params=pltpu.CompilerParams(vmem_limit_bytes=VMEM_LIMIT),
        name=name,
    )

    def run(*operands):
        placed = list(operands)
        for i in range(smem + near, smem + near + far):
            placed[i] = pltpu.with_memory_space_constraint(placed[i], pltpu.HBM)
        for i in range(smem, smem + near):
            placed[i] = pltpu.with_memory_space_constraint(placed[i], pltpu.VMEM)
        return inner(*placed)

    return run


def shape(*dims):
    return pltpu.VMEM(dims, F32)


def sems(count):
    return pltpu.SemaphoreType.DMA((count,))


def like(value):
    return pltpu.VMEM(value.shape, BF16 if value.dtype == ml_dtypes.bfloat16 else F32)


def swap_on(values):
    count = lax.axis_size("patch")
    return lax.ppermute(values, "patch", [(i, i ^ 1) for i in range(count)])


def swap_off(values):
    count = lax.axis_size("patch")
    pairs = [(i, i + 1) for i in range(1, count - 1, 2)]
    return lax.ppermute(values, "patch", pairs + [(j, i) for i, j in pairs])


def swap_frames(values, bit):
    count = lax.axis_size("frames")
    return lax.ppermute(values, "frames", [(i, i ^ bit) for i in range(count)])


def body(object_band, data_band, coeffs, mode_basis, offsets, window_ids, counts):
    columns = object_band.shape[1]
    host = constants()
    const = {name: jnp.asarray(value) for name, value in host.items()}
    room = {name: like(value) for name, value in host.items()}
    halo_room = pltpu.VMEM((HALO, FK, columns), F32)
    pupil_room = [
        pltpu.VMEM((CHUNKS, MODES, CHUNK), F32), pltpu.VMEM((NI, PU * PU), F32), pltpu.VMEM((FK, 1, PC, MODES), F32),
        room["opening"], sems(CHUNKS + 2),
    ]
    wave_given = (coeffs, const["opening"], mode_basis)
    early_matrices = ("pupil_right", "pupil_left", "fwd_left", "fwd_right")
    matrices = [const[name] for name in early_matrices]
    made_early = [shape(PU * NI, LANES)] + [room[name] for name in early_matrices[:2]]
    on_send, off_send, *early = call(
        pack_kernel, [shape(3 * HALO, columns)] * 2 + made_early,
        scratch=[halo_room, halo_room, sems(4), sems(4)] + pupil_room, far=7, name="pack",
    )(object_band, data_band, *wave_given, *matrices[:2])
    on_halo = swap_on(on_send)
    off_halo = swap_off(off_send)
    kept = ("windows", "real_left", "back_left", "back_right")
    pupil, _, _, fwd_left, fwd_right, field, spec, scale, ext, *kept_values = call(
        psf_kernel,
        made_early + [room[name] for name in early_matrices[2:]] + [shape(2 * PP, NI * LANES), shape(PC * PP, 2 * LANES), shape(NI, LANES), shape(1 + FK, HEIGHT, 4 * LANES)]
        + [room[name] for name in kept],
        scratch=[
            pltpu.VMEM((2, PU * NI, LANES), F32), pltpu.VMEM((2 * PU, NI * LANES), F32), pltpu.VMEM((STRIDE, FK, columns), F32),
            sems(8), sems(4),
        ] + pupil_room,
        near=3,
        far=13,
        aliases={i: i for i in range(3)},
        name="psf",
    )(*early, *wave_given, object_band, data_band, *matrices, *[const[name] for name in kept])
    here = dict(zip(kept, kept_values))
    obj_spec, res_spec, centre, on_rim, off_rim = call(
        misfit_kernel,
        [shape(PC * PP, 2 * LANES)] * 2 + [shape(STRIDE, columns), shape(HALO, columns), shape(HALO, columns)],
        scratch=[pltpu.VMEM((1 + FK, HEIGHT, 4 * LANES), F32), pltpu.VMEM((HEIGHT, 4 * LANES), F32)],
        smem=3,
        near=8,
        name="misfit",
    )(
        jnp.transpose(offsets, (0, 2, 1)), window_ids, counts.reshape(1, 1), off_halo, on_halo, spec, ext,
        here["windows"], here["real_left"], fwd_left, fwd_right,
    )
    on_rim = swap_on(on_rim)
    off_rim = swap_off(off_rim)
    spread_grad = call(spread_grad_kernel, shape(2 * PP, PC * LANES), near=4, name="spread_grad")(
        obj_spec, res_spec, fwd_left, fwd_right
    )
    even = lax.axis_index("patch") % 2 == 0
    upper = jnp.where(even, off_rim, on_rim)
    lower = jnp.where(even, on_rim, off_rim)
    rows = jnp.concatenate([centre[:HALO] + upper, centre[HALO : STRIDE - HALO], centre[STRIDE - HALO :] + lower], axis=0)
    rows, spread_grad = lax.optimization_barrier((rows, spread_grad))
    moved = swap_frames(rows, 5) + swap_frames(rows, 4) + swap_frames(rows, 1)
    flat, basis = call(
        phase_grad_kernel, [shape(NI, PU * PU), shape(*mode_basis.shape)],
        scratch=[pltpu.VMEM((2, PU * NI, LANES), F32), sems(1)], near=6, far=1, name="phase_grad",
    )(spread_grad, field, scale, pupil, here["back_left"], here["back_right"], mode_basis)
    rows = rows + moved
    rows, flat = lax.optimization_barrier((rows, flat))
    coeff_grad = call(mode_kernel, jax.ShapeDtypeStruct((FK, 1, PC, MODES), F32), near=2, name="modes")(flat, basis)
    rows = rows + swap_frames(rows, 3)
    return rows, coeff_grad


def solution(mesh):
    in_specs = (
        P("patch", None),
        P("patch", "frames", None),
        P("frames", "patch", None, None),
        P(),
        P("patch", None, None),
        P("patch", None),
        P("patch"),
    )
    out_specs = (P("patch", None), P("frames", "patch", None, None))
    return jax.shard_map(body, mesh=mesh, in_specs=in_specs, out_specs=out_specs, check_vma=False)
```
